32 devices in a mesh: row: 16 (over z, x, core), col: 2 (over y).
Axes of the slice: x: 2, y: 2, z: 4, core: 2. Of those that a mesh axis runs over, the one named last changes fastest.
Arguments:
- row_emb: bfloat16 [16384, 256], P('row'), may hold values from -1.5 to 1.5
- col_emb: bfloat16 [2048, 256], P('col'), may hold values from -1.5 to 1.5
- counts: int32 [2, 16384, 2048], P(None, 'row', 'col'), may hold values from 0 to 2025, as said below
- row_totals: int32 [16384], P('row'), may hold values from 1 to 4096
- col_totals: int32 [2048], P('col'), may hold values from 1 to 4096
- row_ids: int32 [2, 16384], replicated, may hold values from 0 to 16383, as said below
- col_ids: int32 [2, 2048], P(None, 'col'), may hold values from 0 to 2047, as said below
Outputs:
- grad_rows: float32 [16384, 256], P('row')
- grad_cols: float32 [2048, 256], P('col')
The draws below stay inside these ranges and needn't reach their ends.
Inputs may be any that keep to these rules, and one draw needn't show every extreme that they name: `row_ids`: for each step a permutation of 0 to 16383; position p of it holds an item whose id divided by 1024 (rounded down) equals p modulo 16384 / 1024. `col_ids`: for each step and each c, positions c * 1024 to (c + 1) * 1024 - 1 hold a permutation of the items c * 1024 to (c + 1) * 1024 - 1. `counts`: about half of the entries are zero.
All inputs are finite; a program needn't handle non-finite values.
Results may differ from the reference program's by a relative error of at most 0.0037.
Values may be sent and summed in bfloat16 or wider, within the bound.
No kernel may reach another device: no remote copies, remote signals or barrier semaphores. Data moves between devices by JAX's collectives and lax.ppermute only.
A program may use at most 64 MiB of HBM per device.

```python
import math
import jax
import jax.numpy as jnp
from jax import lax

D = 256
BR = 1024
BC = 1024
STEPS = 2
NR = 16384
NC = 2048
N_ROW = 16
N_COL = 2


def draw_counts(key, part):
    shape = (STEPS, NR, NC)
    first = jax.random.fold_in(key, 11)
    second = jax.random.fold_in(key, 12)
    third = jax.random.fold_in(key, 13)
    present = jax.random.randint(first, shape, 0, 2)
    left = jax.random.randint(second, shape, 1, 46)
    right = jax.random.randint(third, shape, 1, 46)
    return (present * left * right).astype(jnp.int32)


def draw_row_totals(key, part):
    left = jax.random.randint(jax.random.fold_in(key, 21), (NR,), 1, 65)
    right = jax.random.randint(jax.random.fold_in(key, 22), (NR,), 1, 65)
    return (left * right).astype(jnp.int32)


def draw_col_totals(key, part):
    left = jax.random.randint(jax.random.fold_in(key, 31), (NC,), 1, 65)
    right = jax.random.randint(jax.random.fold_in(key, 32), (NC,), 1, 65)
    return (left * right).astype(jnp.int32)


def draw_row_ids(key, part):
    owners = NR // BR
    share = BR // owners
    keys = jax.random.split(jax.random.fold_in(key, 41), STEPS * owners)
    perms = jax.vmap(lambda single: jax.random.permutation(single, BR))(keys)
    perms = perms.reshape(STEPS, owners, owners, share)
    placed = jnp.transpose(perms, (0, 2, 3, 1)) + (jnp.arange(owners, dtype=jnp.int32) * BR)[None, None, None, :]
    return placed.reshape(STEPS, NR).astype(jnp.int32)


def draw_col_ids(key, part):
    blocks = NC // BC
    keys = jax.random.split(jax.random.fold_in(key, 51), STEPS * blocks)
    perms = jax.vmap(lambda single: jax.random.permutation(single, BC))(keys)
    perms = perms.reshape(STEPS, blocks, BC) + (jnp.arange(blocks, dtype=jnp.int32) * BC)[None, :, None]
    return perms.reshape(STEPS, NC).astype(jnp.int32)


def steps_of(key, dims, cuts, least, top_value):
    loudness = 1.0
    for position, parts in cuts:
        heights = jax.random.uniform(jax.random.fold_in(jax.random.fold_in(key, 6), position), (parts,), jnp.float32, least / len(cuts), top_value / len(cuts))
        loudness = loudness * jnp.repeat(jnp.exp(heights), dims[position] // parts).reshape((-1,) + (1,) * (len(dims) - 1 - position))
    return loudness


def bell_draw(key, dims, spread, bound, cuts=(), kind=jnp.bfloat16):
    level = steps_of(key, dims, cuts, -0.22, 0.18) if cuts else 1.0
    entries = jax.random.normal(key, dims, jnp.float32) * spread * level
    return jnp.minimum(jnp.maximum(entries, -bound), bound).astype(kind)


def setup_inputs(seed: int = 0) -> dict:
    arg_keys = jax.random.split(jax.random.key(seed), 8)
    return {
        "row_emb": bell_draw(arg_keys[0], (NR, D), 0.25, 1.5, ((0, 16),)),
        "col_emb": bell_draw(arg_keys[1], (NC, D), 0.25, 1.5, ((0, 2),)),
        "counts": draw_counts(jax.random.fold_in(arg_keys[7], 71), 0),
        "row_totals": draw_row_totals(jax.random.fold_in(arg_keys[7], 71), 0),
        "col_totals": draw_col_totals(jax.random.fold_in(arg_keys[7], 71), 0),
        "row_ids": draw_row_ids(jax.random.fold_in(arg_keys[7], 71), 0),
        "col_ids": draw_col_ids(jax.random.fold_in(arg_keys[7], 71), 0),
    }


log_total = 8.0

def block_slope(scores, block_counts, row_log, col_log):
    counted = block_counts.astype(jnp.float32)
    offset = log_total - row_log.astype(jnp.float32)[:, None] - col_log[None, :]
    fitted = (0.1 + 0.25 * jnp.sqrt(counted)) * (scores - jnp.log(jnp.maximum(counted, 1.0)) - offset)
    hinge = jax.nn.sigmoid(scores - offset)
    return jnp.where(block_counts > 0, fitted, hinge)

def reference(row_emb, col_emb, counts, row_totals, col_totals, row_ids, col_ids):
    row_log = jnp.log(row_totals.astype(jnp.float32)).astype(jnp.bfloat16)
    col_log = jnp.log(col_totals.astype(jnp.float32))
    scale = (STEPS * math.sqrt(NR * NC)) ** (-0.5)
    grad_rows = jnp.zeros((NR, D), jnp.float32)
    grad_cols = jnp.zeros((NC, D), jnp.float32)
    for step in range(STEPS):
        for block in range(N_ROW):
            rid = row_ids[step, block * BR:(block + 1) * BR]
            rows_here = row_emb[rid].astype(jnp.float32)
            for column in range(N_COL):
                cid = col_ids[step, column * BC:(column + 1) * BC]
                cols_here = col_emb[cid].astype(jnp.float32)
                scores = jnp.dot(rows_here, cols_here.T, precision=lax.Precision.HIGHEST)
                local = counts[step, block * BR:(block + 1) * BR, column * BC:(column + 1) * BC]
                slope = block_slope(scores, local, row_log[rid], col_log[cid])
                weights = (slope * scale).astype(jnp.bfloat16).astype(jnp.float32)
                grad_rows = grad_rows.at[rid].add(jnp.dot(weights, cols_here, precision=lax.Precision.HIGHEST))
                grad_cols = grad_cols.at[cid].add(jnp.dot(weights.T, rows_here, precision=lax.Precision.HIGHEST))
    return (grad_rows, grad_cols)
```

```python
import functools
import math

import jax
import jax.numpy as jnp
from jax import lax
from jax.experimental import pallas as pl
from jax.experimental.pallas import tpu as pltpu
from jax.sharding import PartitionSpec as P

log_total = 8.0
f32 = jnp.float32
bf16 = jnp.bfloat16
MIB = 1 << 20


def nt(a, b):
    return lax.dot_general(a, b, (((1,), (1,)), ((), ())), preferred_element_type=f32)


def tn(a, b):
    return lax.dot_general(a, b, (((0,), (0,)), ((), ())), preferred_element_type=f32)


def nn(a, b):
    return jnp.dot(a, b, preferred_element_type=f32)


def iota(shape, dim):
    return lax.broadcasted_iota(jnp.int32, shape, dim)


def ones_where(cond):
    return jnp.where(cond, 1.0, 0.0).astype(bf16)


def split_index(ids, size):
    local = ids & (size - 1)
    return (local >> 5).astype(f32).astype(bf16), (local & 31).astype(f32).astype(bf16)


def swap_halves(x, half):
    width = x.shape[1] // 2
    a, b = x[:, :width], x[:, width:]
    first = jnp.where(half == 0, a, b)
    second = jnp.where(half == 0, b, a)
    return jnp.concatenate([first, second], axis=1)


def kernel_call(body, outs, *args, vmem=32, cost=None, **kw):
    return pl.pallas_call(
        body,
        out_shape=outs,
        compiler_params=pltpu.CompilerParams(vmem_limit_bytes=vmem * MIB),
        cost_estimate=cost,
        **kw,
    )(*args)


def cost(flops, nbytes):
    return pl.CostEstimate(flops=int(flops), bytes_accessed=int(nbytes), transcendentals=0)


class Plan:
    def __init__(self, owners, cols, steps, block, width):
        self.owners = owners
        self.cols = cols
        self.steps = steps
        self.block = block
        self.width = width
        self.half = width // 2
        self.chips = owners // 2
        self.share = block // owners
        self.pair = 2 * self.share
        self.far_bit = self.chips // 2
        self.near = [m for m in range(self.chips) if not m & self.far_bit]
        self.far = [m for m in range(self.chips) if m & self.far_bit]
        self.deep = min(4, self.chips)
        self.wide = self.chips // self.deep
        self.msg_rows = steps * self.pair + 16


def fetch_kernel(p, ids_ref, own_ref, oth_ref, tot_own_ref, tot_oth_ref, *msgs):
    r = lax.axis_index("row")
    half = lax.axis_index("col") % 2
    lines = p.steps * p.owners * 8
    group = 128 // p.owners
    hi, lo = split_index(ids_ref[...].reshape(lines, 128), p.block)
    sub = iota((p.pair, 128), 0)
    lane = iota((p.pair, 128), 1)
    owner = r ^ (sub // p.share)
    inner = sub % p.share
    pick = ones_where((lane % p.owners == owner) & (lane // p.owners == inner % group))
    sub2 = iota((p.pair, lines), 0) % p.share
    lane2 = iota((p.pair, lines), 1)
    keep = lane2 % 8 == sub2 // group
    line = iota((lines, 128), 0)
    slot = iota((lines, 128), 1)
    step_ok = line // (p.owners * 8) == slot // p.chips
    dest = (line // 8) % p.owners
    route = ones_where(step_ok & (dest == (r ^ (2 * (slot % p.chips)))))

    def column(digit):
        picked = jnp.where(keep, nt(pick, digit), 0.0).astype(bf16)
        return nn(picked, route)

    index = (column(hi) * 32.0 + column(lo)).astype(jnp.int32)
    logs = jnp.zeros((16, p.chips * p.share), f32)
    log_row = iota((16, p.chips * p.share), 0)
    items = iota((p.share, p.block), 1)
    tables = [swap_halves(own_ref[...], half), swap_halves(oth_ref[...], half)]
    totals = [tot_own_ref, tot_oth_ref]
    for jj in range(2):
        table_log = jnp.log(totals[jj][...].astype(f32)).astype(bf16)
        table_log = jnp.broadcast_to(table_log, (16, p.block))
        for s in range(p.steps):
            pieces = []
            for m in range(p.chips):
                n = s * p.chips + m
                col = index[jj * p.share : (jj + 1) * p.share, n : n + 1]
                pieces.append(ones_where(items == col))
            onehot = jnp.concatenate(pieces, axis=0)
            rows = nn(onehot, tables[jj]).astype(bf16)
            logs = logs + jnp.where(log_row == s * 2 + jj, nt(table_log, onehot), 0.0)
            for m in range(p.chips):
                at = s * p.pair + jj * p.share
                w = msgs[m].shape[1]
                msgs[m][at : at + p.share, :] = rows[m * p.share : (m + 1) * p.share, :w]
    base = p.steps * p.pair
    for m in range(p.chips):
        tile = (m * p.share) // 128 * 128
        msgs[m][base : base + 16, :128] = logs[:, tile : tile + 128].astype(bf16)
        if msgs[m].shape[1] > 128:
            msgs[m][base : base + 16, 128:] = jnp.zeros((16, msgs[m].shape[1] - 128), bf16)


def fetch(p, ids, own, oth, tot_own, tot_oth):
    outs = []
    for m in range(p.chips):
        w = p.half if m & p.far_bit else p.width
        outs.append(jax.ShapeDtypeStruct((p.msg_rows, w), bf16))
    return kernel_call(
        functools.partial(fetch_kernel, p), outs, ids, own, oth, tot_own, tot_oth, vmem=40,
        cost=cost(4 * 2 * 512 * 1024 * 256, 4 * MIB),
    )


def columns_kernel(p, ids_ref, emb_ref, tot_ref, cols_ref, logs_ref):
    half = lax.axis_index("col") % 2
    block = emb_ref.shape[0]
    table = swap_halves(emb_ref[...], half)
    local = (ids_ref[...] & (block - 1)).astype(f32)
    sub8 = iota((8, block), 0)
    stack = jnp.zeros((8, block), f32)
    for s in range(p.steps):
        stack = jnp.where(sub8 == s, jnp.broadcast_to(local[s : s + 1, :], (8, block)), stack)
    index = stack.T.astype(jnp.int32)
    logs = jnp.log(tot_ref[...].astype(f32))
    first = logs.astype(bf16).astype(f32)
    second = (logs - first).astype(bf16).astype(f32)
    third = logs - first - second
    sub16 = iota((16, block), 0)
    digits = jnp.where(sub16 == 0, first, jnp.where(sub16 == 1, second, jnp.where(sub16 == 2, third, 0.0)))
    digits = digits.astype(bf16)
    items = iota((block, block), 1)
    out = jnp.zeros((8, block), f32)
    for s in range(p.steps):
        onehot = ones_where(items == index[:, s : s + 1])
        cols_ref[s] = nn(onehot, table).astype(bf16)
        got = nt(digits, onehot)
        row = got[0:1, :] + got[1:2, :] + got[2:3, :]
        out = jnp.where(sub8 == s, jnp.broadcast_to(row, (8, block)), out)
    logs_ref[...] = out


def columns(p, ids, emb, tot):
    block, width = emb.shape
    outs = [
        jax.ShapeDtypeStruct((p.steps, block, width), bf16),
        jax.ShapeDtypeStruct((8, block), f32),
    ]
    return kernel_call(
        functools.partial(columns_kernel, p), outs, ids, emb, tot, vmem=40,
        cost=cost(2 * 2 * 1024 * 1024 * 256, 2 * MIB),
    )


def factors_kernel(p, scale, counts_ref, gain_ref, shift_ref):
    r = lax.axis_index("row")
    for m in range(p.chips):
        for jj in range(2):
            owner = r ^ (2 * m + jj)
            x = counts_ref[0, pl.ds(owner, p.share, stride=p.owners), :].astype(f32)
            safe = jnp.maximum(x, 1.0)
            root = safe * lax.rsqrt(safe)
            gain = jnp.where(x > 0.0, (0.1 * scale) + (0.25 * scale) * root, 0.0)
            at = (2 * m + jj) * p.share
            gain_ref[0, at : at + p.share, :] = gain
            shift_ref[0, at : at + p.share, :] = jnp.log(safe)


def factors(p, scale, counts):
    steps, rows, width = counts.shape
    tile = 128
    spec = pl.BlockSpec((1, rows, tile), lambda s, t: (s, 0, t))
    shape = jax.ShapeDtypeStruct(counts.shape, f32)
    return kernel_call(
        functools.partial(factors_kernel, p, scale), [shape, shape], counts, vmem=24,
        grid=(steps, width // tile), in_specs=[spec], out_specs=[spec, spec],
        cost=cost(40 * counts.size, 12 * counts.size),
    )


def grads_kernel(p, scale, masks, split, *refs):
    count = len(masks)
    n_in = count * (2 if split else 1)
    msgs = refs[:n_in]
    cols_ref, col_logs_ref, gain_ref, shift_ref = refs[n_in : n_in + 4]
    keep_ref, side_ref, core_ref, diag_ref, acc_ref = refs[n_in + 4 : n_in + 9]
    rows_ref, logs_ref = refs[n_in + 9 :]
    s, t = pl.program_id(0), pl.program_id(1)
    base = p.steps * p.pair

    @pl.when((s == 0) & (t == 0))
    def _():
        for i, m in enumerate(masks):
            own = msgs[i]
            logs = own[base : base + 16, :128].astype(f32).T
            off = (m * p.share) % 128
            for step in range(p.steps):
                dst = i * p.pair
                src = step * p.pair
                if split:
                    other = msgs[count + i]
                    rows_ref[step, dst : dst + p.pair, : p.half] = own[src : src + p.pair, :]
                    rows_ref[step, dst : dst + p.pair, p.half :] = other[src : src + p.pair, :]
                else:
                    rows_ref[step, dst : dst + p.pair, :] = own[src : src + p.pair, :]
                for jj in range(2):
                    col = logs[off : off + p.share, step * 2 + jj : step * 2 + jj + 1]
                    at = dst + jj * p.share
                    logs_ref[step, at : at + p.share, :] = jnp.broadcast_to(
                        col - log_total, (p.share, 128)
                    )

    tile = gain_ref.shape[1]
    at = pl.multiple_of(t * tile, tile)
    x = rows_ref[s, pl.ds(at, tile), :]
    cols = cols_ref[s]
    row_logs = logs_ref[s, pl.ds(at, tile), :][:, :1]
    col_logs = col_logs_ref[pl.ds(s, 1), :]
    z = nt(x, cols) + (row_logs + col_logs)
    gain = gain_ref[0]
    fitted = gain * (z - shift_ref[0])
    hinge = (0.5 * scale) * jnp.tanh(0.5 * z) + (0.5 * scale)
    weights = jnp.where(gain > 0.0, fitted, hinge).astype(bf16)
    g = nn(weights, cols)
    for i in range(tile // p.pair):
        lo = i * p.pair
        mid = lo + p.share
        hi = mid + p.share
        keep_ref[0, i] = g[lo:mid, : p.half]
        side_ref[0, i] = g[lo:mid, p.half :].astype(bf16)
        core_ref[0, i] = g[mid:hi, : p.half].astype(bf16)
        diag_ref[0, i] = g[mid:hi, p.half :].astype(bf16)
    c = tn(weights, x)

    @pl.when(t == 0)
    def _():
        acc_ref[0] = c

    @pl.when(t != 0)
    def _():
        acc_ref[0] += c


def grads(p, scale, masks, split, msgs, cols, col_logs, gain, shift):
    count = len(masks)
    block = cols.shape[1]
    tile = min(256, count * p.pair)
    per = tile // p.pair
    tiles = count * p.pair // tile
    first = masks[0] * p.pair // tile
    whole = lambda a: pl.BlockSpec(a.shape, lambda s, t: (0,) * a.ndim)
    factor = pl.BlockSpec((1, tile, block), lambda s, t: (s, first + t, 0))
    piece = pl.BlockSpec((1, per, p.share, p.half), lambda s, t: (s, t, 0, 0))
    shape = (p.steps, count, p.share, p.half)
    outs = [jax.ShapeDtypeStruct(shape, f32)] + [jax.ShapeDtypeStruct(shape, bf16)] * 3
    outs.append(jax.ShapeDtypeStruct((p.steps, block, p.width), f32))
    return kernel_call(
        functools.partial(grads_kernel, p, scale, masks, split), outs,
        *msgs, cols, col_logs, gain, shift, vmem=48,
        grid=(p.steps, tiles),
        in_specs=[whole(a) for a in (*msgs, cols, col_logs)] + [factor, factor],
        out_specs=[piece] * 4 + [pl.BlockSpec((1, block, p.width), lambda s, t: (s, 0, 0))],
        scratch_shapes=[
            pltpu.VMEM((p.steps, count * p.pair, p.width), bf16),
            pltpu.VMEM((p.steps, count * p.pair, 128), f32),
        ],
        cost=cost(3 * 2 * p.steps * 512 * 1024 * 256, 10 * MIB),
    )


def merge_kernel(p, keep_ref, side_ref, core_ref, diag_ref, *outs):
    for i, out in enumerate(outs):
        for s in range(p.steps):
            out[s, 0] = (keep_ref[s, i] + side_ref[s, i].astype(f32)).astype(bf16)
            out[s, 1] = (core_ref[s, i].astype(f32) + diag_ref[s, i].astype(f32)).astype(bf16)


def merge(p, keep, side, core, diag):
    outs = [jax.ShapeDtypeStruct((p.steps, 2, p.share, p.half), bf16)] * keep.shape[1]
    return kernel_call(
        functools.partial(merge_kernel, p), outs, keep, side, core, diag, vmem=16,
        cost=cost(MIB, 2 * MIB),
    )


def collect_kernel(p, ids_ref, *refs):
    msgs, out_ref = refs[:-1], refs[-1]
    r = lax.axis_index("row")
    lines = p.steps * p.owners * 8
    group = 128 // p.owners
    slots = p.steps * p.chips
    hi, lo = split_index(ids_ref[...].reshape(lines, 128), p.block)
    lane = iota((128, p.pair), 0)
    inner = iota((128, p.pair), 1) % p.share
    pick = ones_where((lane % p.owners == r) & (lane // p.owners == inner % group))
    line = iota((lines, p.pair), 0)
    keep = line % 8 == (iota((lines, p.pair), 1) % p.share) // group
    slot = iota((slots, lines), 0)
    line2 = iota((slots, lines), 1)
    step_ok = line2 // (p.owners * 8) == slot // p.chips
    source = (line2 // 8) % p.owners
    routes = [ones_where(step_ok & (source == (r ^ (2 * (slot % p.chips) + jj)))) for jj in range(2)]

    def row(digit):
        picked = jnp.where(keep, nn(digit, pick), 0.0).astype(bf16)
        first = nn(routes[0], picked)
        second = nn(routes[1], picked)
        return jnp.where(iota((slots, p.pair), 1) < p.share, first, second)

    index = (row(hi) * 32.0 + row(lo)).astype(jnp.int32)
    items = iota((p.block, p.pair), 0)
    acc = jnp.zeros((p.block, p.half), f32)
    for s in range(p.steps):
        for m in range(0, p.chips, 2):
            n = s * p.chips + m
            onehot = jnp.concatenate(
                [ones_where(items == index[n + k : n + k + 1, :]) for k in range(2)], axis=1
            )
            rows = jnp.concatenate([msgs[m + k][s].reshape(p.pair, p.half) for k in range(2)], axis=0)
            acc = acc + nn(onehot, rows)
    out_ref[...] = acc.astype(bf16)


def collect(p, ids, msgs):
    return kernel_call(
        functools.partial(collect_kernel, p),
        jax.ShapeDtypeStruct((p.block, p.half), bf16), ids, *msgs, vmem=32,
        cost=cost(2 * 1024 * 2048 * 256, 2 * MIB),
    )


def join_kernel(own_ref, oth_ref, out_ref):
    half = lax.axis_index("col") % 2
    a, b = own_ref[...].astype(f32), oth_ref[...].astype(f32)
    width = a.shape[1]
    out_ref[:, :width] = jnp.where(half == 0, a, b)
    out_ref[:, width:] = jnp.where(half == 0, b, a)


def place_kernel(p, ids_ref, near_ref, far_ref, mine_ref, other_ref, acc_ref):
    r = lax.axis_index("row")
    block = near_ref.shape[1]
    local = ids_ref[...] & (block - 1)
    items = iota((block, block), 0)
    for s in range(p.steps):
        total = near_ref[s] + far_ref[s]
        top = total.astype(bf16)
        rest = (total - top.astype(f32)).astype(bf16)
        onehot = ones_where(items == local[s : s + 1, :])
        term = nn(onehot, top) + nn(onehot, rest)
        if s == 0:
            acc_ref[...] = term
        else:
            acc_ref[...] += term
    part = block // 2
    mine_ref[...] = acc_ref[pl.ds(pl.multiple_of((r % 2) * part, part), part), :]
    other_ref[...] = acc_ref[pl.ds(pl.multiple_of((1 - r % 2) * part, part), part), :]


def place(p, ids, near, far):
    block, width = near.shape[1:]
    out = jax.ShapeDtypeStruct((block // 2, width), f32)
    return kernel_call(
        functools.partial(place_kernel, p), [out, out], ids, near, far, vmem=40,
        scratch_shapes=[pltpu.VMEM((block, width), f32)],
        cost=cost(4 * 2 * 1024 * 1024 * 256, 5 * MIB),
    )


def spread_kernel(parts, stride, count, *refs):
    mine, arrived = refs[0], refs[1 : 1 + count]
    outs, acc_ref = refs[1 + count : -1], refs[-1]
    here = (lax.axis_index("row") // stride) % parts
    total = mine[...]
    for a in arrived:
        total = total + a[...].astype(f32)
    acc_ref[...] = total
    size = outs[0].shape[0]
    for k, out in enumerate(outs):
        at = pl.multiple_of((here ^ k) * size, size)
        out[...] = acc_ref[pl.ds(at, size), :].astype(out.dtype)


def spread(parts, stride, mine, arrived):
    rows, width = mine.shape
    size = rows // parts
    outs = [jax.ShapeDtypeStruct((size, width), bf16 if (parts == 1 or k) else f32) for k in range(parts)]
    return kernel_call(
        functools.partial(spread_kernel, parts, stride, len(arrived)), outs, mine, *arrived, vmem=16,
        scratch_shapes=[pltpu.VMEM((rows, width), f32)],
        cost=cost(MIB, MIB),
    )


def gather_kernel(parts, stride, unswap, *refs):
    pieces, out = refs[:-1], refs[-1]
    here = (lax.axis_index("row") // stride) % parts
    half = lax.axis_index("col") % 2
    size = pieces[0].shape[0]
    for k, piece in enumerate(pieces):
        at = pl.multiple_of((here ^ k) * size, size)
        value = piece[...].astype(out.dtype)
        if unswap:
            value = swap_halves(value, half)
        out[pl.ds(at, size), :] = value


def gather(stride, pieces, dtype=bf16, unswap=False):
    parts = len(pieces)
    rows, width = pieces[0].shape
    return kernel_call(
        functools.partial(gather_kernel, parts, stride, unswap),
        jax.ShapeDtypeStruct((parts * rows, width), dtype), *pieces, vmem=16,
        cost=cost(MIB, MIB),
    )


def local(row_emb, col_emb, counts, row_totals, col_totals, row_ids, col_ids):
    owners = lax.axis_size("row")
    cols_n = lax.axis_size("col")
    block, width = row_emb.shape
    block_cols = col_emb.shape[0]
    steps = counts.shape[0]
    p = Plan(owners, cols_n, steps, block, width)
    scale = (steps * math.sqrt(owners * block * cols_n * block_cols)) ** (-0.5)

    def row_swap(x, mask):
        return lax.ppermute(x, "row", [(i, i ^ mask) for i in range(owners)])

    def col_swap(x, mask=1):
        return lax.ppermute(x, "col", [(i, i ^ mask) for i in range(cols_n)])

    def diag_swap(x):
        perm = [
            (i * cols_n + j, (i ^ 1) * cols_n + (j ^ 1)) for i in range(owners) for j in range(cols_n)
        ]
        return lax.ppermute(x, ("row", "col"), perm)

    ids = row_ids.reshape(steps, owners * block // 128, 128)
    totals = row_totals.reshape(1, block)
    msgs = fetch(p, ids, row_emb, row_swap(row_emb, 1), totals, row_swap(totals, 1))
    got = [msgs[m] if m == 0 else row_swap(msgs[m], 2 * m) for m in range(p.chips)]
    cols, col_logs = columns(p, col_ids, col_emb, col_totals.reshape(1, block_cols))
    gain, shift = factors(p, scale, counts)
    near_in = [got[m] for m in p.near]
    far_in = [got[m] for m in p.far] + [col_swap(got[m]) for m in p.far]

    back = {}
    sums = []
    for masks, split, inputs in ((p.near, False, near_in), (p.far, True, far_in)):
        keep, side, core, diag, acc = grads(p, scale, masks, split, inputs, cols, col_logs, gain, shift)
        sums.append(acc)
        outs = merge(p, keep, col_swap(side), row_swap(core, 1), diag_swap(diag))
        for m, out in zip(masks, outs):
            back[m] = out if m == 0 else row_swap(out, 2 * m)

    mine, other = place(p, col_ids, *sums)
    arrived = [row_swap(other, 1)]
    for parts, stride in ((p.wide, 2), (p.deep, 2 * p.wide)):
        mine, *others = spread(parts, stride, mine, arrived)
        arrived = [row_swap(o, (k + 1) * stride) for k, o in enumerate(others)]
    (piece,) = spread(1, 1, mine, arrived)
    for parts, stride in ((p.deep, 2 * p.wide), (p.wide, 2)):
        piece = gather(stride, [piece] + [row_swap(piece, k * stride) for k in range(1, parts)])
    grad_cols = gather(1, [piece, row_swap(piece, 1)], f32, True)

    rows = collect(p, ids, [back[m] for m in range(p.chips)])
    if cols_n > 2:
        total = rows.astype(f32)
        for mask in range(2, cols_n, 2):
            total = total + col_swap(rows, mask).astype(f32)
        rows = total.astype(bf16)
    grad_rows = kernel_call(
        join_kernel, jax.ShapeDtypeStruct((block, width), f32), rows, col_swap(rows), vmem=16,
        cost=cost(MIB, 2 * MIB),
    )
    return grad_rows, grad_cols


def solution(mesh):
    in_specs = (
        P("row", None),
        P("col", None),
        P(None, "row", "col"),
        P("row"),
        P("col"),
        P(),
        P(None, "col"),
    )
    out_specs = (P("row", None), P("col", None))
    return jax.shard_map(local, mesh=mesh, in_specs=in_specs, out_specs=out_specs, check_vma=False)
```

```python
import functools
import math

import jax
import jax.numpy as jnp
from jax import lax
from jax.experimental import pallas as pl
from jax.experimental.pallas import tpu as pltpu
from jax.sharding import PartitionSpec as P

log_total = 8.0
f32 = jnp.float32
bf16 = jnp.bfloat16
MIB = 1 << 20


def nt(a, b):
    return lax.dot_general(a, b, (((1,), (1,)), ((), ())), preferred_element_type=f32)


def tn(a, b):
    return lax.dot_general(a, b, (((0,), (0,)), ((), ())), preferred_element_type=f32)


def nn(a, b):
    return jnp.dot(a, b, preferred_element_type=f32)


def iota(shape, dim):
    return lax.broadcasted_iota(jnp.int32, shape, dim)


def ones_where(cond):
    return jnp.where(cond, 1.0, 0.0).astype(bf16)


def split_index(ids, size):
    local = ids & (size - 1)
    return (local >> 5).astype(f32).astype(bf16), (local & 31).astype(f32).astype(bf16)


def kernel_call(body, outs, *args, vmem=32, cost=None, **kw):
    return pl.pallas_call(
        body,
        out_shape=outs,
        compiler_params=pltpu.CompilerParams(vmem_limit_bytes=vmem * MIB),
        cost_estimate=cost,
        **kw,
    )(*args)


def cost(flops, nbytes):
    return pl.CostEstimate(flops=1, bytes_accessed=1, transcendentals=0)


def anywhere(items):
    return [pl.BlockSpec(memory_space=pl.ANY)] * len(items)


def in_vmem(items):
    return [pl.BlockSpec(memory_space=pltpu.VMEM)] * len(items)


class Plan:
    def __init__(self, owners, steps, block, width):
        self.owners = owners
        self.steps = steps
        self.block = block
        self.width = width
        self.chips = owners // 2
        self.groups = self.chips // 4
        self.share = block // owners
        self.pair = 2 * self.share
        self.deep = min(4, self.chips)
        self.wide = self.chips // self.deep
        self.rows = steps * self.pair


def turn(t):
    return ((t & 1) * 2) ^ ((t >> 1) * 3)


def position():
    r = lax.axis_index("row")
    half = lax.axis_index("col") % 2
    return r, half, turn(2 * (r % 2) + half)


def fetch_kernel(p, ids_ref, own_ref, oth_ref, tot_own_ref, tot_oth_ref, *msgs):
    r, half, mine = position()
    lines = p.steps * p.owners * 8
    group = 128 // p.owners
    count = 2 * len(msgs)
    hi, lo = split_index(ids_ref[...].reshape(lines, 128), p.block)
    sub = iota((p.pair, 128), 0)
    lane = iota((p.pair, 128), 1)
    owner = r ^ (sub // p.share)
    inner = sub % p.share
    pick = ones_where((lane % p.owners == owner) & (lane // p.owners == inner % group))
    sub2 = iota((p.pair, lines), 0) % p.share
    lane2 = iota((p.pair, lines), 1)
    keep = lane2 % 8 == sub2 // group
    line = iota((lines, 128), 0)
    slot = iota((lines, 128), 1)
    step_ok = line // (p.owners * 8) == slot // count
    dest = (line // 8) % p.owners
    mask = (4 * ((slot % count) // 2)) ^ mine
    route = ones_where(step_ok & (dest == (r ^ (2 * mask + slot % 2))))

    def column(digit):
        picked = jnp.where(keep, nt(pick, digit), 0.0).astype(bf16)
        return nn(picked, route)

    index = (column(hi) * 32.0 + column(lo)).astype(jnp.int32)
    logs = jnp.zeros((16, count * p.share), f32)
    log_row = iota((16, count * p.share), 0)
    items = iota((p.share, p.block), 1)
    tables = [own_ref, oth_ref]
    totals = [tot_own_ref, tot_oth_ref]
    for jj in range(2):
        table_log = jnp.log(totals[jj][...].astype(f32)).astype(bf16)
        table_log = jnp.broadcast_to(table_log, (16, p.block))
        for s in range(p.steps):
            pieces = []
            for e in range(count):
                n = s * count + e
                col = index[jj * p.share : (jj + 1) * p.share, n : n + 1]
                pieces.append(ones_where(items == col))
            onehot = jnp.concatenate(pieces, axis=0)
            rows = nn(onehot, tables[jj][...]).astype(bf16)
            logs = logs + jnp.where(log_row == s * 2 + jj, nt(table_log, onehot), 0.0)
            for e in range(count):
                at = e % 2 * p.rows + s * p.pair + jj * p.share
                msgs[e // 2][at : at + p.share, :] = rows[e * p.share : (e + 1) * p.share, :]
    for g, msg in enumerate(msgs):
        tile = (2 * g * p.share) // 128 * 128
        msg[2 * p.rows : 2 * p.rows + 16, :128] = logs[:, tile : tile + 128].astype(bf16)
        msg[2 * p.rows : 2 * p.rows + 16, 128:] = jnp.zeros((16, p.width - 128), bf16)


def fetch(p, ids, own, oth, tot_own, tot_oth):
    outs = [jax.ShapeDtypeStruct((2 * p.rows + 16, p.width), bf16)] * p.groups
    return kernel_call(
        functools.partial(fetch_kernel, p), outs, ids, own, oth, tot_own, tot_oth, vmem=12,
        cost=cost(4 * 2 * 256 * 1024 * 256, 4 * MIB),
    )


def columns_kernel(p, ids_ref, emb_ref, tot_ref, row_ids_ref, *refs):
    cols_ref, logs_ref, index_ref = refs[-3:]
    block = emb_ref.shape[0]
    table = emb_ref[...]
    local = (ids_ref[...] & (block - 1)).astype(f32)
    sub8 = iota((8, block), 0)
    stack = jnp.zeros((8, block), f32)
    for s in range(p.steps):
        stack = jnp.where(sub8 == s, jnp.broadcast_to(local[s : s + 1, :], (8, block)), stack)
    index = stack.T.astype(jnp.int32)
    logs = jnp.log(tot_ref[...].astype(f32))
    first = logs.astype(bf16).astype(f32)
    second = (logs - first).astype(bf16).astype(f32)
    third = logs - first - second
    sub16 = iota((16, block), 0)
    digits = jnp.where(sub16 == 0, first, jnp.where(sub16 == 1, second, jnp.where(sub16 == 2, third, 0.0)))
    digits = digits.astype(bf16)
    items = iota((block, block), 1)
    out = jnp.zeros((8, block), f32)
    for s in range(p.steps):
        onehot = ones_where(items == index[:, s : s + 1])
        cols_ref[s] = nn(onehot, table).astype(bf16)
        got = nt(digits, onehot)
        row = got[0:1, :] + got[1:2, :] + got[2:3, :]
        out = jnp.where(sub8 == s, jnp.broadcast_to(row, (8, block)), out)
    logs_ref[...] = out

    r, half, mine = position()
    lines = p.steps * p.owners * 8
    group = 128 // p.owners
    slots = p.groups * 4 * p.steps
    hi, lo = split_index(row_ids_ref[...].reshape(lines, 128), p.block)
    lane = iota((128, p.pair), 0)
    inner = iota((128, p.pair), 1) % p.share
    pick = ones_where((lane % p.owners == r) & (lane // p.owners == inner % group))
    keep = iota((lines, p.pair), 0) % 8 == (iota((lines, p.pair), 1) % p.share) // group
    slot = iota((slots, lines), 0)
    line = iota((slots, lines), 1)
    step_ok = line // (p.owners * 8) == slot % p.steps
    q = (slot // p.steps) % 4
    mask = (4 * (slot // (4 * p.steps))) ^ mine ^ turn(q)
    routes = [
        ones_where(step_ok & ((line // 8) % p.owners == (r ^ (2 * mask + (k ^ (q // 2)))))) for k in range(2)
    ]

    def row_of(digit):
        picked = jnp.where(keep, nn(digit, pick), 0.0).astype(bf16)
        return jnp.where(iota((slots, p.pair), 1) < p.share, nn(routes[0], picked), nn(routes[1], picked))

    index_ref[...] = (row_of(hi) * 32.0 + row_of(lo)).astype(jnp.int32)


def columns(p, ids, emb, tot, row_ids, after):
    block, width = emb.shape
    outs = [
        jax.ShapeDtypeStruct((p.steps, block, width), bf16),
        jax.ShapeDtypeStruct((8, block), f32),
        jax.ShapeDtypeStruct((p.groups * 4 * p.steps, p.pair), jnp.int32),
    ]
    args = (ids, emb, tot, row_ids)
    return kernel_call(
        functools.partial(columns_kernel, p), outs, *args, *after, vmem=12,
        in_specs=in_vmem(args) + anywhere(after),
        cost=cost(2 * 2 * 1024 * 1024 * 256, 2 * MIB),
    )


def factors_kernel(p, scale, step, counts_ref, *refs):
    gain_ref, shift_ref, buf_ref, sems = refs[-4:]
    r, half, mine = position()
    slots = buf_ref.shape[0]
    tiles = counts_ref.shape[2] // 128

    def copy(k):
        src = counts_ref.at[step, :, pl.ds(k * 128, 128)]
        return pltpu.make_async_copy(src, buf_ref.at[k % slots], sems.at[k % slots])

    for k in range(slots - 1):
        copy(k).start()
    for k in range(tiles):
        if k + slots - 1 < tiles:
            copy(k + slots - 1).start()
        copy(k).wait()
        for g in range(p.groups):
            for q in range(4):
                for jj in range(2):
                    owner = r ^ (2 * ((4 * g) ^ turn(q) ^ mine) + (jj ^ (q // 2)))
                    x = buf_ref[k % slots, pl.ds(owner, p.share, stride=p.owners), :].astype(f32)
                    safe = jnp.maximum(x, 1.0)
                    root = safe * lax.rsqrt(safe)
                    at = ((g * 4 + q) * 2 + jj) * p.share
                    gain = jnp.where(x > 0.0, (0.1 * scale) + (0.25 * scale) * root, 0.0)
                    gain_ref[at : at + p.share, k * 128 : k * 128 + 128] = gain
                    shift_ref[at : at + p.share, k * 128 : k * 128 + 128] = jnp.log(safe)


def factors(p, scale, counts, step, after, vmem):
    shape = jax.ShapeDtypeStruct(counts.shape[1:], f32)
    slots = 4
    return kernel_call(
        functools.partial(factors_kernel, p, scale, step), [shape, shape], counts, *after, vmem=vmem,
        in_specs=anywhere((counts, *after)), out_specs=in_vmem((shape, shape)),
        scratch_shapes=[
            pltpu.VMEM((slots, counts.shape[1], 128), jnp.int32),
            pltpu.SemaphoreType.DMA((slots,)),
        ],
        cost=cost(40 * counts.size / 2, 12 * counts.size / 2),
    )


def grads_kernel(p, scale, first, has_acc, *refs):
    msgs = refs[:4]
    cols_ref, col_logs_ref = refs[4:6]
    factor_refs = refs[6 : 6 + 2 * p.steps]
    outs, acc_ref = refs[-4:-1], refs[-1]
    before = refs[6 + 2 * p.steps] if has_acc else None
    targets = [(outs[0], 0), (outs[2], 0), (outs[1], 0), (outs[2], p.rows)]
    group = max(1, 256 // p.pair)
    for s in range(p.steps):
        cols = cols_ref[s]
        col_logs = col_logs_ref[s : s + 1, :] - log_total
        for q0 in range(0, 4, group):
            members = range(q0, min(q0 + group, 4))
            pieces, row_logs = [], []
            for q in members:
                lo = q // 2 * p.rows + s * p.pair
                pieces.append(msgs[q][lo : lo + p.pair, :])
                logs = msgs[q][2 * p.rows : 2 * p.rows + 16, :128].astype(f32).T
                off = ((first // 2 + q // 2) * p.share) % 128
                for jj in range(2):
                    row_logs.append(logs[off : off + p.share, s * 2 + jj : s * 2 + jj + 1])
            x = jnp.concatenate(pieces, axis=0)
            rows = x.shape[0]
            z = nt(x, cols) + (jnp.concatenate(row_logs, axis=0) + col_logs)
            at = (first + q0) * p.pair
            gain = factor_refs[2 * s][at : at + rows, :]
            fitted = gain * (z - factor_refs[2 * s + 1][at : at + rows, :])
            hinge = (0.5 * scale) * jnp.tanh(0.5 * z) + (0.5 * scale)
            weights = jnp.where(gain > 0.0, fitted, hinge).astype(bf16)
            g = nn(weights, cols)
            for k, q in enumerate(members):
                out, lo = targets[q]
                lo += s * p.pair
                out[lo : lo + p.pair, :] = g[k * p.pair : (k + 1) * p.pair].astype(out.dtype)
            c = tn(x, weights)
            if q0 == 0:
                acc_ref[s] = before[s] + c if has_acc else c
            else:
                acc_ref[s] += c


def grads(p, scale, first, msgs, cols, col_logs, factor, acc=None):
    block = cols.shape[1]
    stay = jax.ShapeDtypeStruct((p.rows, p.width), f32)
    outs = [stay, stay, jax.ShapeDtypeStruct((2 * p.rows, p.width), bf16)]
    outs.append(jax.ShapeDtypeStruct((p.steps, p.width, block), f32))
    args = (*msgs, cols, col_logs, *factor) + (() if acc is None else (acc,))
    return kernel_call(
        functools.partial(grads_kernel, p, scale, first, acc is not None), outs, *args, vmem=24,
        cost=cost(3 * 2 * p.steps * 512 * 1024 * 256, 10 * MIB),
    )


def meet_kernel(p, own_ref, pass_ref, got_ref, *refs):
    own_out, pass_out = refs[-2:]
    own_out[...] = (own_ref[...] + got_ref[: p.rows, :].astype(f32)).astype(bf16)
    pass_out[...] = (pass_ref[...] + got_ref[p.rows :, :].astype(f32)).astype(bf16)


def meet(p, own, passed, got, after=()):
    outs = [jax.ShapeDtypeStruct((p.rows, p.width), bf16)] * 2
    args = (own, passed, got)
    return kernel_call(
        functools.partial(meet_kernel, p), outs, *args, *after, vmem=12,
        in_specs=in_vmem(args) + anywhere(after), cost=cost(MIB, 2 * MIB),
    )


def merge_kernel(p, own_ref, core_ref, *refs):
    out = refs[-1]
    for d in range(2):
        for s in range(p.steps):
            src = slice(s * p.pair + d * p.share, s * p.pair + (d + 1) * p.share)
            lo = d * p.rows + s * p.pair
            out[lo : lo + p.share, :] = own_ref[src, :]
            out[lo + p.share : lo + p.pair, :] = core_ref[src, :]


def merge(p, own, core, after=()):
    args = (own, core)
    return kernel_call(
        functools.partial(merge_kernel, p), jax.ShapeDtypeStruct((2 * p.rows, p.width), bf16), *args, *after,
        vmem=12, in_specs=in_vmem(args) + anywhere(after), cost=cost(MIB, 2 * MIB),
    )


def collect_kernel(p, first, has_acc, index_ref, *refs):
    msgs, out_ref = refs[:2], refs[-1]
    items = iota((p.block, p.pair), 0)
    total = refs[2][...] if has_acc else None
    base = first % 4 // 2 * p.rows
    for s in range(p.steps):
        at = [(first + i) * p.steps + s for i in range(2)]
        onehot = jnp.concatenate([ones_where(items == index_ref[k : k + 1, :]) for k in at], axis=1)
        lo = base + s * p.pair
        rows = jnp.concatenate([m[lo : lo + p.pair, :] for m in msgs], axis=0)
        term = nn(onehot, rows)
        total = term if total is None else total + term
    out_ref[...] = total


def collect(p, first, index, msgs, acc=None):
    args = (index, *msgs) + (() if acc is None else (acc,))
    return kernel_call(
        functools.partial(collect_kernel, p, first, acc is not None),
        jax.ShapeDtypeStruct((p.block, p.width), f32), *args, vmem=12,
        cost=cost(2 * 1024 * 512 * 256, 2 * MIB),
    )


def place_kernel(p, ids_ref, sum_ref, mine_ref, other_ref, acc_ref):
    r = lax.axis_index("row")
    block = sum_ref.shape[2]
    local = ids_ref[...] & (block - 1)
    items = iota((block, block), 0)
    for s in range(p.steps):
        total = sum_ref[s]
        top = total.astype(bf16)
        rest = (total - top.astype(f32)).astype(bf16)
        onehot = ones_where(items == local[s : s + 1, :])
        term = nt(onehot, top) + nt(onehot, rest)
        if s == 0:
            acc_ref[...] = term
        else:
            acc_ref[...] += term
    part = block // 2
    mine_ref[...] = acc_ref[pl.ds(pl.multiple_of((r % 2) * part, part), part), :]
    other_ref[...] = acc_ref[pl.ds(pl.multiple_of((1 - r % 2) * part, part), part), :]


def place(p, ids, sums):
    width, block = sums.shape[1:]
    out = jax.ShapeDtypeStruct((block // 2, width), f32)
    return kernel_call(
        functools.partial(place_kernel, p), [out, out], ids, sums, vmem=12,
        scratch_shapes=[pltpu.VMEM((block, width), f32)],
        cost=cost(4 * 2 * 1024 * 1024 * 256, 5 * MIB),
    )


def spread_kernel(parts, stride, count, *refs):
    mine, arrived = refs[0], refs[1 : 1 + count]
    outs, acc_ref = refs[1 + count : -1], refs[-1]
    here = (lax.axis_index("row") // stride) % parts
    total = mine[...]
    for a in arrived:
        total = total + a[...].astype(f32)
    acc_ref[...] = total
    size = outs[0].shape[0]
    for k, out in enumerate(outs):
        at = pl.multiple_of((here ^ k) * size, size)
        out[...] = acc_ref[pl.ds(at, size), :].astype(out.dtype)


def spread(parts, stride, mine, arrived):
    rows, width = mine.shape
    size = rows // parts
    outs = [jax.ShapeDtypeStruct((size, width), bf16 if (parts == 1 or k) else f32) for k in range(parts)]
    return kernel_call(
        functools.partial(spread_kernel, parts, stride, len(arrived)), outs, mine, *arrived, vmem=16,
        scratch_shapes=[pltpu.VMEM((rows, width), f32)],
        cost=cost(MIB, MIB),
    )


def add_kernel(a_ref, b_ref, out_ref):
    out_ref[...] = (a_ref[...].astype(f32) + b_ref[...].astype(f32)).astype(out_ref.dtype)


def add(a, b):
    return kernel_call(add_kernel, jax.ShapeDtypeStruct(a.shape, a.dtype), a, b, vmem=12, cost=cost(MIB, MIB))


def gather_kernel(parts, stride, *refs):
    pieces, out = refs[:-1], refs[-1]
    here = (lax.axis_index("row") // stride) % parts
    size = pieces[0].shape[0]
    for k, piece in enumerate(pieces):
        at = pl.multiple_of((here ^ k) * size, size)
        value = piece[...].astype(out.dtype)
        out[pl.ds(at, size), :] = value


def gather(stride, pieces, dtype=bf16):
    parts = len(pieces)
    rows, width = pieces[0].shape
    return kernel_call(
        functools.partial(gather_kernel, parts, stride),
        jax.ShapeDtypeStruct((parts * rows, width), dtype), *pieces, vmem=16,
        cost=cost(MIB, MIB),
    )


def local(row_emb, col_emb, counts, row_totals, col_totals, row_ids, col_ids):
    owners = lax.axis_size("row")
    cols_n = lax.axis_size("col")
    block, width = row_emb.shape
    block_cols = col_emb.shape[0]
    steps = counts.shape[0]
    p = Plan(owners, steps, block, width)
    scale = (steps * math.sqrt(owners * block * cols_n * block_cols)) ** (-0.5)

    def row_swap(x, mask):
        return lax.ppermute(x, "row", [(i, i ^ mask) for i in range(owners)])

    def col_swap(x, mask=1):
        return lax.ppermute(x, "col", [(i, i ^ mask) for i in range(cols_n)])

    def grid_swap(x, mask_of):
        perm = []
        for i in range(owners):
            for j in range(cols_n):
                row_mask, col_mask = mask_of(2 * (i % 2) + j % 2)
                perm.append((i * cols_n + j, (i ^ row_mask) * cols_n + (j ^ col_mask)))
        return lax.ppermute(x, ("row", "col"), perm)

    def tie(x, *others):
        return lax.optimization_barrier((x, *others))[0]

    def carry(x, group):
        return grid_swap(x, lambda t: (2 * ((4 * group) ^ turn(t)), 0))

    ids = row_ids.reshape(steps, owners * block // 128, 128)
    totals = row_totals.reshape(1, block)
    msgs = fetch(p, ids, row_emb, row_swap(row_emb, 1), totals, row_swap(totals, 1))
    got = [carry(m, g) for g, m in enumerate(msgs)]
    cols, col_logs, index = columns(
        p, col_ids, col_emb, col_totals.reshape(1, block_cols), ids, (msgs[0],)
    )

    factor = []
    last = col_logs
    landed = [None] * p.groups
    for s in range(steps):
        factor += factors(p, scale, counts, s, (last,), 44 if s == 0 else 38)
        last = factor[-1]
        for g in range(p.groups):
            if s == min(g, steps - 1):
                here = tie(got[g], last)
                landed[g] = (here, col_swap(here))

    acc = None
    ready = None
    arrived = None
    rows = None
    end = p.groups - 1
    for g in range(p.groups):
        here, there = landed[g]
        four = (here, there, row_swap(here, 1), row_swap(there, 1))
        own, passed, send, acc = grads(p, scale, 4 * g, four, cols, col_logs, factor, acc)
        own, passed = meet(p, own, passed, col_swap(send), () if ready is None else (ready,))
        ready = merge(p, own, row_swap(passed, 1), () if arrived is None else (arrived,))
        arrived = carry(ready, g)
        if g == end:
            arrived = tie(arrived, there_back) if g else arrived
            far_landed = arrived
        there_back = col_swap(arrived)
        for k, pair in enumerate(((arrived, there_back), (row_swap(arrived, 1), row_swap(there_back, 1)))):
            rows = collect(p, 4 * g + 2 * k, index, pair, rows)

    mine, other = place(p, col_ids, acc)
    mine, *others = spread(p.wide, 2, mine, [row_swap(other, 1)])
    (piece,) = spread(1, 1, mine, [row_swap(o, (k + 1) * 2) for k, o in enumerate(others)])
    stride = 2 * p.wide
    while stride < owners:
        piece = add(piece, row_swap(piece, stride))
        stride *= 2
    piece = tie(piece, far_landed)
    piece = gather(2, [piece] + [row_swap(piece, k * 2) for k in range(1, p.wide)])
    piece = tie(piece, there_back)
    grad_cols = gather(1, [piece, row_swap(piece, 1)], f32)

    if cols_n > 2:
        total = rows
        for mask in range(2, cols_n, 2):
            total = total + col_swap(rows.astype(bf16), mask).astype(f32)
        rows = total
    return rows, grad_cols


def solution(mesh):
    in_specs = (
        P("row", None),
        P("col", None),
        P(None, "row", "col"),
        P("row"),
        P("col"),
        P(),
        P(None, "col"),
    )
    out_specs = (P("row", None), P("col", None))
    return jax.shard_map(local, mesh=mesh, in_specs=in_specs, out_specs=out_specs, check_vma=False)
```

```python
import functools
import math

import jax
import jax.numpy as jnp
from jax import lax
from jax.experimental import pallas as pl
from jax.experimental.pallas import tpu as pltpu
from jax.sharding import PartitionSpec as P

log_total = 8.0
f32 = jnp.float32
bf16 = jnp.bfloat16
MIB = 1 << 20
C = dict(meet=0, merge=0, collect=1, place=0, nsend=1, mfar=0, farland=0, ztie=1, ctie=1, nmerge=0, nmeet=0, place1=0, sp2=0, ncol=0, ytime=0, nlate=2, rtie=1, one=1, yfirst=0)


def nt(a, b):
    return lax.dot_general(a, b, (((1,), (1,)), ((), ())), preferred_element_type=f32)


def tn(a, b):
    return lax.dot_general(a, b, (((0,), (0,)), ((), ())), preferred_element_type=f32)


def nn(a, b):
    return jnp.dot(a, b, preferred_element_type=f32)


def iota(shape, dim):
    return lax.broadcasted_iota(jnp.int32, shape, dim)


def ones_where(cond):
    return jnp.where(cond, 1.0, 0.0).astype(bf16)


def split_index(ids, size):
    local = ids & (size - 1)
    return (local >> 5).astype(f32).astype(bf16), (local & 31).astype(f32).astype(bf16)


def kernel_call(body, outs, *args, vmem=32, cost=None, **kw):
    return pl.pallas_call(
        body,
        out_shape=outs,
        compiler_params=pltpu.CompilerParams(vmem_limit_bytes=vmem * MIB),
        cost_estimate=cost,
        **kw,
    )(*args)


def cost(us):
    return pl.CostEstimate(flops=int(us * 1.1e9), bytes_accessed=1, transcendentals=0)


def anywhere(items):
    return [pl.BlockSpec(memory_space=pl.ANY)] * len(items)


def in_vmem(items):
    return [pl.BlockSpec(memory_space=pltpu.VMEM)] * len(items)


class Plan:
    def __init__(self, owners, steps, block, width):
        self.owners = owners
        self.steps = steps
        self.block = block
        self.width = width
        self.chips = owners // 2
        self.groups = self.chips // 4
        self.share = block // owners
        self.pair = 2 * self.share
        self.deep = min(4, self.chips)
        self.wide = self.chips // self.deep
        self.slots = 2 * self.groups + 2


def turn(t):
    return ((t & 1) * 2) ^ ((t >> 1) * 3)


def position():
    r = lax.axis_index("row")
    half = lax.axis_index("col") % 2
    return r, half, turn(2 * (r % 2) + half)


def fetched(p, g, q, r, mine):
    if g:
        return (4 * g) ^ turn(q) ^ mine, q // 2
    return q, 0


def fetch_kernel(p, ids_ref, own_ref, oth_ref, tot_own_ref, tot_oth_ref, *msgs):
    r, half, mine = position()
    lines = p.steps * p.owners * 8
    group = 128 // p.owners
    count = p.slots
    hi, lo = split_index(ids_ref[...].reshape(lines, 128), p.block)
    sub = iota((p.pair, 128), 0)
    lane = iota((p.pair, 128), 1)
    owner = r ^ (sub // p.share)
    inner = sub % p.share
    pick = ones_where((lane % p.owners == owner) & (lane // p.owners == inner % group))
    sub2 = iota((p.pair, lines), 0) % p.share
    lane2 = iota((p.pair, lines), 1)
    keep = lane2 % 8 == sub2 // group
    line = iota((lines, 128), 0)
    slot = iota((lines, 128), 1)
    step_ok = line // (p.owners * 8) == slot // count
    dest = (line // 8) % p.owners
    e = slot % count
    far = 2 * ((4 * (e // 2 - 1)) ^ mine) + e % 2
    route = ones_where(step_ok & (dest == (r ^ jnp.where(e < 4, 2 * e, far))))

    def column(digit):
        picked = jnp.where(keep, nt(pick, digit), 0.0).astype(bf16)
        return nn(picked, route)

    index = (column(hi) * 32.0 + column(lo)).astype(jnp.int32)
    logs = jnp.zeros((16, count * p.share), f32)
    log_row = iota((16, count * p.share), 0)
    items = iota((p.share, p.block), 1)
    tables = [own_ref, oth_ref]
    totals = [tot_own_ref, tot_oth_ref]
    for jj in range(2):
        table_log = jnp.log(totals[jj][...].astype(f32)).astype(bf16)
        table_log = jnp.broadcast_to(table_log, (16, p.block))
        for s in range(p.steps):
            pieces = []
            for e in range(count):
                n = s * count + e
                col = index[jj * p.share : (jj + 1) * p.share, n : n + 1]
                pieces.append(ones_where(items == col))
            onehot = jnp.concatenate(pieces, axis=0)
            rows = nn(onehot, tables[jj][...]).astype(bf16)
            logs = logs + jnp.where(log_row == s * 2 + jj, nt(table_log, onehot), 0.0)
            for e in range(count):
                piece = rows[e * p.share : (e + 1) * p.share, :]
                if e < 4:
                    msg, at = msgs[e], s * p.pair
                else:
                    msg, at = msgs[2 + e // 2], (e % 2 * p.steps + s) * p.pair
                msg[at + jj * p.share : at + (jj + 1) * p.share, :] = piece
    for k, msg in enumerate(msgs):
        e = k if k < 4 else 2 * k - 4
        tile = (e * p.share) // 128 * 128
        end = msg.shape[0] - 16
        wide = min(128, count * p.share - tile)
        msg[end : end + 16, :] = jnp.zeros((16, p.width), bf16)
        msg[end : end + 16, :wide] = logs[:, tile : tile + wide].astype(bf16)


def fetch(p, ids, own, oth, tot_own, tot_oth):
    n = p.steps * p.pair
    outs = [jax.ShapeDtypeStruct((k * n + 16, p.width), bf16) for k in [1] * 4 + [2] * (p.groups - 1)]
    return kernel_call(
        functools.partial(fetch_kernel, p), outs, ids, own, oth, tot_own, tot_oth, vmem=12,
        cost=cost(3),
    )


def columns_kernel(p, ids_ref, emb_ref, tot_ref, row_ids_ref, *refs):
    cols_ref, logs_ref, index_ref = refs[-3:]
    block = emb_ref.shape[0]
    table = emb_ref[...]
    local = (ids_ref[...] & (block - 1)).astype(f32)
    sub8 = iota((8, block), 0)
    stack = jnp.zeros((8, block), f32)
    for s in range(p.steps):
        stack = jnp.where(sub8 == s, jnp.broadcast_to(local[s : s + 1, :], (8, block)), stack)
    index = stack.T.astype(jnp.int32)
    logs = jnp.log(tot_ref[...].astype(f32))
    first = logs.astype(bf16).astype(f32)
    second = (logs - first).astype(bf16).astype(f32)
    third = logs - first - second
    sub16 = iota((16, block), 0)
    digits = jnp.where(sub16 == 0, first, jnp.where(sub16 == 1, second, jnp.where(sub16 == 2, third, 0.0)))
    digits = digits.astype(bf16)
    items = iota((block, block), 1)
    out = jnp.zeros((8, block), f32)
    for s in range(p.steps):
        onehot = ones_where(items == index[:, s : s + 1])
        cols_ref[s] = nn(onehot, table).astype(bf16)
        got = nt(digits, onehot)
        row = got[0:1, :] + got[1:2, :] + got[2:3, :]
        out = jnp.where(sub8 == s, jnp.broadcast_to(row, (8, block)), out)
    logs_ref[...] = out

    r, half, mine = position()
    lines = p.steps * p.owners * 8
    group = 128 // p.owners
    slots = p.groups * 4 * p.steps
    hi, lo = split_index(row_ids_ref[...].reshape(lines, 128), p.block)
    lane = iota((128, p.pair), 0)
    inner = iota((128, p.pair), 1) % p.share
    pick = ones_where((lane % p.owners == r) & (lane // p.owners == inner % group))
    keep = iota((lines, p.pair), 0) % 8 == (iota((lines, p.pair), 1) % p.share) // group
    slot = iota((slots, lines), 0)
    line = iota((slots, lines), 1)
    step_ok = line // (p.owners * 8) == slot % p.steps
    q = (slot // p.steps) % 4
    mask = (4 * (slot // (4 * p.steps))) ^ mine ^ turn(q)
    routes = [
        ones_where(step_ok & ((line // 8) % p.owners == (r ^ (2 * mask + (k ^ (q // 2)))))) for k in range(2)
    ]

    def row_of(digit):
        picked = jnp.where(keep, nn(digit, pick), 0.0).astype(bf16)
        return jnp.where(iota((slots, p.pair), 1) < p.share, nn(routes[0], picked), nn(routes[1], picked))

    index_ref[...] = (row_of(hi) * 32.0 + row_of(lo)).astype(jnp.int32)


def columns(p, ids, emb, tot, row_ids, after):
    block, width = emb.shape
    outs = [
        jax.ShapeDtypeStruct((p.steps, block, width), bf16),
        jax.ShapeDtypeStruct((8, block), f32),
        jax.ShapeDtypeStruct((p.groups * 4 * p.steps, p.pair), jnp.int32),
    ]
    args = (ids, emb, tot, row_ids)
    return kernel_call(
        functools.partial(columns_kernel, p), outs, *args, *after, vmem=12,
        in_specs=in_vmem(args) + anywhere(after),
        cost=cost(3),
    )


def pack_kernel(n, a_ref, b_ref, out_ref):
    out_ref[:n, :] = a_ref[n : 2 * n, :]
    out_ref[n : 2 * n, :] = b_ref[n : 2 * n, :]
    if out_ref.shape[0] > 2 * n:
        out_ref[2 * n : 2 * n + 16, :] = a_ref[2 * n :, :]
        out_ref[2 * n + 16 :, :] = b_ref[2 * n :, :]


def pack(a, b):
    rows, width = a.shape
    more = rows % 32
    n = (rows - more) // 2
    return kernel_call(
        functools.partial(pack_kernel, n), jax.ShapeDtypeStruct((2 * n + 2 * more, width), bf16), a, b, vmem=12,
        cost=cost(0),
    )


def factors_kernel(p, scale, step, counts_ref, *refs):
    gain_ref, shift_ref, buf_ref, sems = refs[-4:]
    r, half, mine = position()
    slots = buf_ref.shape[0]
    tiles = counts_ref.shape[2] // 128

    def copy(k):
        src = counts_ref.at[step, :, pl.ds(k * 128, 128)]
        return pltpu.make_async_copy(src, buf_ref.at[k % slots], sems.at[k % slots])

    for k in range(slots - 1):
        copy(k).start()
    for k in range(tiles):
        if k + slots - 1 < tiles:
            copy(k + slots - 1).start()
        copy(k).wait()
        for g in range(p.groups):
            for q in range(4):
                for jj in range(2):
                    mask, swapped = fetched(p, g, q, r, mine)
                    owner = r ^ (2 * mask + (jj ^ swapped))
                    x = buf_ref[k % slots, pl.ds(owner, p.share, stride=p.owners), :].astype(f32)
                    safe = jnp.maximum(x, 1.0)
                    root = safe * lax.rsqrt(safe)
                    at = ((g * 4 + q) * 2 + jj) * p.share
                    gain = jnp.where(x > 0.0, (0.1 * scale) + (0.25 * scale) * root, 0.0)
                    gain_ref[at : at + p.share, k * 128 : k * 128 + 128] = gain
                    shift_ref[at : at + p.share, k * 128 : k * 128 + 128] = jnp.log(safe)


def factors(p, scale, counts, step, after, vmem):
    shape = jax.ShapeDtypeStruct(counts.shape[1:], f32)
    slots = 4
    return kernel_call(
        functools.partial(factors_kernel, p, scale, step), [shape, shape], counts, *after, vmem=vmem,
        in_specs=anywhere((counts, *after)), out_specs=in_vmem((shape, shape)),
        scratch_shapes=[
            pltpu.VMEM((slots, counts.shape[1], 128), jnp.int32),
            pltpu.SemaphoreType.DMA((slots,)),
        ],
        cost=cost(0),
    )


def grads_kernel(p, scale, g, steps, *refs):
    n = len(steps)
    m = 3 if g else 4
    msgs, refs = refs[:m], refs[m:]
    size = n * p.pair
    if g:
        here, there, crossed = msgs
        sources = [(here, 0, 2 * size), (there, 0, 2 * size), (crossed, 0, 2 * size), (crossed, size, 2 * size + 16)]
    else:
        sources = [(msg, 0, size) for msg in msgs]
    cols_ref, col_logs_ref = refs[:2]
    factor_refs = refs[2 : 2 + 2 * n]
    outs, acc_refs, rows_ref = refs[-4 - n : -1 - n], refs[-1 - n : -1], refs[-1]
    befores = refs[2 + 2 * n : 2 + 3 * n] if g else None
    r, half, mine = position()
    targets = [(outs[0], 0), (outs[2], 0), (outs[1], 0), (outs[2], n * p.pair)]
    group = max(1, 256 // p.pair)
    for i, s in enumerate(steps):
        cols = cols_ref[s]
        col_logs = col_logs_ref[s : s + 1, :] - log_total
        for q0 in range(0, 4, group):
            members = range(q0, min(q0 + group, 4))
            pieces, row_logs = [], []
            for q in members:
                msg, lo, end = sources[q]
                lo += i * p.pair
                pieces.append(msg[lo : lo + p.pair, :])
                logs = msg[end : end + 16, :128].astype(f32).T
                e = 2 * (g + 1) + q // 2 if g else q
                off = (e * p.share) % 128
                for jj in range(2):
                    row_logs.append(logs[off : off + p.share, s * 2 + jj : s * 2 + jj + 1])
            x = jnp.concatenate(pieces, axis=0)
            rows = x.shape[0]
            z = nt(x, cols) + (jnp.concatenate(row_logs, axis=0) + col_logs)
            at = (4 * g + q0) * p.pair
            gain = factor_refs[2 * i][at : at + rows, :]
            fitted = gain * (z - factor_refs[2 * i + 1][at : at + rows, :])
            hinge = (0.5 * scale) * jnp.tanh(0.5 * z) + (0.5 * scale)
            weights = jnp.where(gain > 0.0, fitted, hinge).astype(bf16)
            got = nn(weights, cols)
            if g:
                for k, q in enumerate(members):
                    out, lo = targets[q]
                    lo += i * p.pair
                    out[lo : lo + p.pair, :] = got[k * p.pair : (k + 1) * p.pair].astype(out.dtype)
            else:
                rows_ref[q0 * p.pair : q0 * p.pair + rows, :] = got
            c = tn(x, weights)
            if q0 == 0:
                acc_refs[i][...] = befores[i][...] + c if g else c
            else:
                acc_refs[i][...] += c
        if not g:
            for q, (out, lo) in enumerate(targets):
                mask = mine ^ turn(q)
                for k in range(2):
                    at = pl.multiple_of(mask * p.pair + (k ^ (q // 2)) * p.share, p.share)
                    to = lo + i * p.pair + k * p.share
                    out[to : to + p.share, :] = rows_ref[pl.ds(at, p.share), :].astype(out.dtype)


def grads(p, scale, g, steps, msgs, cols, col_logs, factor, acc=()):
    block = cols.shape[1]
    n = len(steps) * p.pair
    stay = jax.ShapeDtypeStruct((n, p.width), f32)
    outs = [stay, stay, jax.ShapeDtypeStruct((2 * n, p.width), bf16)]
    outs += [jax.ShapeDtypeStruct((p.width, block), f32)] * len(steps)
    args = (*msgs, cols, col_logs, *factor, *acc)
    return kernel_call(
        functools.partial(grads_kernel, p, scale, g, steps), outs, *args, vmem=14,
        scratch_shapes=[pltpu.VMEM((4 * p.pair, p.width), f32)],
        cost=cost(0),
    )


def meet_kernel(own_ref, pass_ref, got_ref, *refs):
    own_out, pass_out = refs[-2:]
    n = own_ref.shape[0]
    own_out[...] = (own_ref[...] + got_ref[:n, :].astype(f32)).astype(bf16)
    pass_out[...] = (pass_ref[...] + got_ref[n:, :].astype(f32)).astype(bf16)


def meet(own, passed, got, after=()):
    outs = [jax.ShapeDtypeStruct(own.shape, bf16)] * 2
    args = (own, passed, got)
    return kernel_call(
        meet_kernel, outs, *args, *after, vmem=12, in_specs=in_vmem(args) + anywhere(after), cost=cost(C['meet'])
    )


def merge_kernel(p, own_ref, core_ref, *refs):
    out = refs[-1]
    n = own_ref.shape[0]
    for d in range(2):
        for at in range(0, n, p.pair):
            src = slice(at + d * p.share, at + (d + 1) * p.share)
            lo = d * n + at
            out[lo : lo + p.share, :] = own_ref[src, :]
            out[lo + p.share : lo + p.pair, :] = core_ref[src, :]


def merge(p, own, core, after=()):
    args = (own, core)
    return kernel_call(
        functools.partial(merge_kernel, p),
        jax.ShapeDtypeStruct((2 * own.shape[0], p.width), bf16), *args, *after,
        vmem=12, in_specs=in_vmem(args) + anywhere(after), cost=cost(C['merge']),
    )


def collect_kernel(p, first, steps, has_acc, index_ref, *refs):
    msgs, out_ref = refs[:2], refs[-1]
    bases = (0, first % 4 // 2)
    items = iota((p.block, p.pair), 0)
    total = refs[2][...] if has_acc else None
    for i, s in enumerate(steps):
        at = [(first + k) * p.steps + s for k in range(2)]
        onehot = jnp.concatenate([ones_where(items == index_ref[k : k + 1, :]) for k in at], axis=1)
        lo = [(base * len(steps) + i) * p.pair for base in bases]
        rows = jnp.concatenate([m[k : k + p.pair, :] for m, k in zip(msgs, lo)], axis=0)
        term = nn(onehot, rows)
        total = term if total is None else total + term
    out_ref[...] = total


def collect(p, first, steps, index, msgs, acc=None):
    args = (index, *msgs) + (() if acc is None else (acc,))
    return kernel_call(
        functools.partial(collect_kernel, p, first, steps, acc is not None),
        jax.ShapeDtypeStruct((p.block, p.width), f32), *args, vmem=12,
        cost=cost(C['collect']),
    )


def finish_kernel(p, first, steps, index_ref, a_ref, b_ref, acc_ref, mine_ref, other_ref, rows_ref, cols_ref):
    half = mine_ref.shape[0]
    core = lax.axis_index("row") % 2
    cols_ref[pl.ds(pl.multiple_of(core * half, half), half), :] = mine_ref[...].astype(f32)
    cols_ref[pl.ds(pl.multiple_of((1 - core) * half, half), half), :] = other_ref[...].astype(f32)
    collect_kernel(p, first, steps, True, index_ref, a_ref, b_ref, acc_ref, rows_ref)


def finish(p, first, steps, index, msgs, acc, mine, other):
    outs = [
        jax.ShapeDtypeStruct((p.block, p.width), f32),
        jax.ShapeDtypeStruct((2 * mine.shape[0], p.width), f32),
    ]
    return kernel_call(
        functools.partial(finish_kernel, p, first, steps), outs, index, *msgs, acc, mine, other, vmem=16,
        cost=cost(0),
    )


def place_kernel(step, final, ids_ref, sum_ref, *refs):
    r = lax.axis_index("row")
    block = sum_ref.shape[1]
    local = ids_ref[...] & (block - 1)
    items = iota((block, block), 0)
    total = sum_ref[...]
    top = total.astype(bf16)
    rest = (total - top.astype(f32)).astype(bf16)
    onehot = ones_where(items == local[step : step + 1, :])
    term = nt(onehot, top) + nt(onehot, rest)
    if step:
        term = term + refs[0][...]
    if not final:
        refs[-1][...] = term
        return
    mine_ref, top_ref, rest_ref, acc_ref = refs[-4:]
    acc_ref[...] = term
    part = block // 2
    mine_ref[...] = acc_ref[pl.ds(pl.multiple_of((r % 2) * part, part), part), :]
    other = acc_ref[pl.ds(pl.multiple_of((1 - r % 2) * part, part), part), :]
    top_ref[...] = other.astype(bf16)
    rest_ref[...] = (other - other.astype(bf16).astype(f32)).astype(bf16)


def place(step, final, ids, sums, acc=(), after=()):
    width, block = sums.shape
    if final:
        outs = [jax.ShapeDtypeStruct((block // 2, width), kind) for kind in (f32, bf16, bf16)]
        scratch = [pltpu.VMEM((block, width), f32)]
    else:
        outs = [jax.ShapeDtypeStruct((block, width), f32)]
        scratch = []
    return kernel_call(
        functools.partial(place_kernel, step, final), outs, ids, sums, *acc, *after, vmem=12,
        in_specs=in_vmem((ids, sums, *acc)) + anywhere(after),
        scratch_shapes=scratch,
        cost=cost(C['place']),
    )


def spread_kernel(parts, stride, count, after, *refs):
    mine, arrived = refs[0], refs[1 : 1 + count]
    outs, acc_ref = refs[1 + count + after : -1], refs[-1]
    here = (lax.axis_index("row") // stride) % parts
    total = mine[...]
    for a in arrived:
        total = total + a[...].astype(f32)
    acc_ref[...] = total
    size = outs[0].shape[0]
    for k, out in enumerate(outs):
        at = pl.multiple_of((here ^ k) * size, size)
        out[...] = acc_ref[pl.ds(at, size), :].astype(out.dtype)


def spread(parts, stride, mine, arrived, after=()):
    rows, width = mine.shape
    size = rows // parts
    outs = [jax.ShapeDtypeStruct((size, width), bf16 if (parts == 1 or k) else f32) for k in range(parts)]
    return kernel_call(
        functools.partial(spread_kernel, parts, stride, len(arrived), len(after)), outs, mine, *arrived, *after,
        vmem=16, in_specs=in_vmem((mine, *arrived)) + anywhere(after),
        scratch_shapes=[pltpu.VMEM((rows, width), f32)],
        cost=cost(0),
    )


def add_kernel(a_ref, b_ref, out_ref):
    out_ref[...] = (a_ref[...].astype(f32) + b_ref[...].astype(f32)).astype(out_ref.dtype)


def add(a, b):
    return kernel_call(add_kernel, jax.ShapeDtypeStruct(a.shape, a.dtype), a, b, vmem=12, cost=cost(0))


def gather_kernel(parts, stride, *refs):
    pieces, out = refs[:-1], refs[-1]
    here = (lax.axis_index("row") // stride) % parts
    size = pieces[0].shape[0]
    for k, piece in enumerate(pieces):
        at = pl.multiple_of((here ^ k) * size, size)
        value = piece[...].astype(out.dtype)
        out[pl.ds(at, size), :] = value


def gather(stride, pieces, dtype=bf16):
    parts = len(pieces)
    rows, width = pieces[0].shape
    return kernel_call(
        functools.partial(gather_kernel, parts, stride),
        jax.ShapeDtypeStruct((parts * rows, width), dtype), *pieces, vmem=16,
        cost=cost(0),
    )


def local(row_emb, col_emb, counts, row_totals, col_totals, row_ids, col_ids):
    owners = lax.axis_size("row")
    cols_n = lax.axis_size("col")
    block, width = row_emb.shape
    block_cols = col_emb.shape[0]
    steps = counts.shape[0]
    p = Plan(owners, steps, block, width)
    scale = (steps * math.sqrt(owners * block * cols_n * block_cols)) ** (-0.5)

    def row_swap(x, mask):
        return lax.ppermute(x, "row", [(i, i ^ mask) for i in range(owners)])

    def col_swap(x, mask=1):
        return lax.ppermute(x, "col", [(i, i ^ mask) for i in range(cols_n)])

    def grid_swap(x, mask_of):
        perm = []
        for i in range(owners):
            for j in range(cols_n):
                row_mask, col_mask = mask_of(2 * (i % 2) + j % 2)
                perm.append((i * cols_n + j, (i ^ row_mask) * cols_n + (j ^ col_mask)))
        return lax.ppermute(x, ("row", "col"), perm)

    def tie(x, *others):
        return lax.optimization_barrier((x, *others))[0]

    def carry(x, group):
        return grid_swap(x, lambda t: (2 * ((4 * group) ^ turn(t)), 0))

    ids = row_ids.reshape(steps, owners * block // 128, 128)
    totals = row_totals.reshape(1, block)
    msgs = fetch(p, ids, row_emb, row_swap(row_emb, 1), totals, row_swap(totals, 1))
    far = [carry(msgs[3 + g], g) for g in range(1, p.groups)]
    near = [msgs[0]] + [row_swap(msgs[k], 2 * k) for k in range(1, 4)]
    cols, col_logs, index = columns(
        p, col_ids, col_emb, col_totals.reshape(1, block_cols), ids, (msgs[0],)
    )

    every = tuple(range(steps))
    factor = []
    last = (col_logs,)
    for s in every:
        factor += factors(p, scale, counts, s, last, 44 if s == 0 else 38)
        last = (factor[-1],)
        if s == C['ytime']:
            far = [tie(x, factor[-1], *near[1:]) for x in far]
            last = (*last, *far)
    near[1] = tie(near[1], *last)

    *term, acc0, acc1 = grads(p, scale, 0, every, near, cols, col_logs, factor)
    terms = [term]
    sums = [acc0, acc1]
    crossed = []
    for g in range(1, p.groups):
        here = far[g - 1]
        there = tie(col_swap(here), acc0)
        crossed.append(there)
        four = (here, there, row_swap(pack(here, there), 1))
        *term, acc0, acc1 = grads(p, scale, g, every, four, cols, col_logs, factor, sums)
        sums = [acc0, acc1]
        terms.append(term)

    def pick(flag, *xs):
        return xs if flag else ()

    met = [col_swap(t[2] if g or not C['nsend'] else tie(t[2], *crossed)) for g, t in enumerate(terms)]
    placed = ()
    for s in every:
        final = s + 1 == steps
        placed = place(
            s, final, col_ids, sums[s], placed,
            pick(final and C['place1'] & 1, met[0]) + pick(final and C['place1'] & 2, met[-1]),
        )
    mine, *rest = placed
    mine, *others = spread(p.wide, 2, mine, [row_swap(x, 1) for x in rest])

    end = p.groups - 1
    both = [None] * p.groups
    for g in (range(end, -1, -1) if C['nmeet'] else range(p.groups)):
        own, passed, _ = terms[g]
        both[g] = meet(
            own, passed, met[g], pick(g and C['mfar'] == 1, mine) + pick(not g and C['nmeet'], both[-1] and both[-1][0]) + pick(not g and C['nlate'] == 1, sums[0]) + pick(not g and C['nlate'] == 2, placed[0])
        )
    parcels = [None] * p.groups
    for g in (range(end, -1, -1) if C['nmerge'] else range(p.groups)):
        own, passed = both[g]
        parcels[g] = merge(
            p, own, row_swap(passed, 1), pick(g and C['mfar'] == 2, mine) + pick(not g and C['nmerge'], parcels[-1])
        )
    (piece,) = spread(
        1, 1, mine, [row_swap(o, (k + 1) * 2) for k, o in enumerate(others)], pick(C['sp2'], parcels[-1])
    )

    rows = None
    there = None
    for g in range(p.groups):
        here = carry(parcels[g], g)
        if g and C['farland']:
            here = tie(here, there, *pick(C['ncol'], rows))
        there = col_swap(here)
        rows = collect(p, 4 * g, every, index, (here, there), rows)
        other = pack(here, there)
        if C['rtie'] and g == end:
            other = tie(other, early)
        other = row_swap(other, 1)
        early = rows
        if g < end or not C['one']:
            rows = early = collect(p, 4 * g + 2, every, index, (other, other), rows)

    stride = 2 * p.wide
    while stride < owners:
        piece = add(piece, row_swap(piece, stride))
        stride *= 2
    if C['ztie']:
        piece = tie(piece, here)
    piece = gather(2, [piece] + [row_swap(piece, k * 2) for k in range(1, p.wide)])
    if C['ctie']:
        piece = tie(piece, there)
    if C['one']:
        rows, grad_cols = finish(p, 4 * end + 2, every, index, (other, other), rows, piece, row_swap(piece, 1))
    else:
        grad_cols = gather(1, [piece, row_swap(piece, 1)], f32)

    if cols_n > 2:
        total = rows
        for mask in range(2, cols_n, 2):
            total = total + col_swap(rows.astype(bf16), mask).astype(f32)
        rows = total
    return rows, grad_cols


def solution(mesh):
    in_specs = (
        P("row", None),
        P("col", None),
        P(None, "row", "col"),
        P("row"),
        P("col"),
        P(),
        P(None, "col"),
    )
    out_specs = (P("row", None), P("col", None))
    return jax.shard_map(local, mesh=mesh, in_specs=in_specs, out_specs=out_specs, check_vma=False)
```

```python
import functools
import math

import jax
import jax.numpy as jnp
from jax import lax
from jax.experimental import pallas as pl
from jax.experimental.pallas import tpu as pltpu
from jax.sharding import PartitionSpec as P

log_total = 8.0
f32 = jnp.float32
bf16 = jnp.bfloat16
MIB = 1 << 20


def nt(a, b):
    return lax.dot_general(a, b, (((1,), (1,)), ((), ())), preferred_element_type=f32)


def tn(a, b):
    return lax.dot_general(a, b, (((0,), (0,)), ((), ())), preferred_element_type=f32)


def nn(a, b):
    return jnp.dot(a, b, preferred_element_type=f32)


def iota(shape, dim):
    return lax.broadcasted_iota(jnp.int32, shape, dim)


def ones_where(cond):
    return jnp.where(cond, 1.0, 0.0).astype(bf16)


def split_index(ids, size):
    local = ids & (size - 1)
    return (local >> 5).astype(f32).astype(bf16), (local & 31).astype(f32).astype(bf16)


def kernel_call(body, outs, *args, vmem=32, cost=None, **kw):
    return pl.pallas_call(
        body,
        out_shape=outs,
        compiler_params=pltpu.CompilerParams(vmem_limit_bytes=vmem * MIB),
        cost_estimate=cost,
        **kw,
    )(*args)


def cost(us):
    return pl.CostEstimate(flops=int(us * 1.1e9), bytes_accessed=1, transcendentals=0)


def anywhere(items):
    return [pl.BlockSpec(memory_space=pl.ANY)] * len(items)


def in_vmem(items):
    return [pl.BlockSpec(memory_space=pltpu.VMEM)] * len(items)


class Plan:
    def __init__(self, owners, steps, block, width):
        self.owners = owners
        self.steps = steps
        self.block = block
        self.width = width
        self.chips = owners // 2
        self.groups = self.chips // 4
        self.share = block // owners
        self.pair = 2 * self.share
        self.deep = min(4, self.chips)
        self.wide = self.chips // self.deep
        self.slots = 2 * self.groups + 2


def turn(t):
    return ((t & 1) * 2) ^ ((t >> 1) * 3)


def position():
    r = lax.axis_index("row")
    half = lax.axis_index("col") % 2
    return r, half, turn(2 * (r % 2) + half)


def fetched(p, g, q, r, mine):
    if g:
        return (4 * g) ^ turn(q) ^ mine, q // 2
    return q, 0


def fetch_kernel(p, ids_ref, own_ref, oth_ref, tot_own_ref, tot_oth_ref, *msgs):
    r, half, mine = position()
    lines = p.steps * p.owners * 8
    group = 128 // p.owners
    count = p.slots
    hi, lo = split_index(ids_ref[...].reshape(lines, 128), p.block)
    sub = iota((p.pair, 128), 0)
    lane = iota((p.pair, 128), 1)
    owner = r ^ (sub // p.share)
    inner = sub % p.share
    pick = ones_where((lane % p.owners == owner) & (lane // p.owners == inner % group))
    sub2 = iota((p.pair, lines), 0) % p.share
    lane2 = iota((p.pair, lines), 1)
    keep = lane2 % 8 == sub2 // group
    line = iota((lines, 128), 0)
    slot = iota((lines, 128), 1)
    step_ok = line // (p.owners * 8) == slot // count
    dest = (line // 8) % p.owners
    e = slot % count
    far = 2 * ((4 * (e // 2 - 1)) ^ mine) + e % 2
    route = ones_where(step_ok & (dest == (r ^ jnp.where(e < 4, 2 * e, far))))

    def column(digit):
        picked = jnp.where(keep, nt(pick, digit), 0.0).astype(bf16)
        return nn(picked, route)

    index = (column(hi) * 32.0 + column(lo)).astype(jnp.int32)
    logs = jnp.zeros((16, count * p.share), f32)
    log_row = iota((16, count * p.share), 0)
    items = iota((p.share, p.block), 1)
    tables = [own_ref, oth_ref]
    totals = [tot_own_ref, tot_oth_ref]
    for jj in range(2):
        table_log = jnp.log(totals[jj][...].astype(f32)).astype(bf16)
        table_log = jnp.broadcast_to(table_log, (16, p.block))
        for s in range(p.steps):
            pieces = []
            for e in range(count):
                n = s * count + e
                col = index[jj * p.share : (jj + 1) * p.share, n : n + 1]
                pieces.append(ones_where(items == col))
            onehot = jnp.concatenate(pieces, axis=0)
            rows = nn(onehot, tables[jj][...]).astype(bf16)
            logs = logs + jnp.where(log_row == s * 2 + jj, nt(table_log, onehot), 0.0)
            for e in range(count):
                piece = rows[e * p.share : (e + 1) * p.share, :]
                if e < 4:
                    msg, at = msgs[e], s * p.pair
                else:
                    msg, at = msgs[2 + e // 2], (e % 2 * p.steps + s) * p.pair
                msg[at + jj * p.share : at + (jj + 1) * p.share, :] = piece
    for k, msg in enumerate(msgs):
        e = k if k < 4 else 2 * k - 4
        tile = (e * p.share) // 128 * 128
        end = msg.shape[0] - 16
        wide = min(128, count * p.share - tile)
        msg[end : end + 16, :] = jnp.zeros((16, p.width), bf16)
        msg[end : end + 16, :wide] = logs[:, tile : tile + wide].astype(bf16)


def fetch(p, ids, own, oth, tot_own, tot_oth):
    n = p.steps * p.pair
    outs = [jax.ShapeDtypeStruct((k * n + 16, p.width), bf16) for k in [1] * 4 + [2] * (p.groups - 1)]
    return kernel_call(
        functools.partial(fetch_kernel, p), outs, ids, own, oth, tot_own, tot_oth, vmem=12,
        cost=cost(3),
    )


def columns_kernel(p, ids_ref, emb_ref, tot_ref, row_ids_ref, *refs):
    cols_ref, logs_ref, index_ref = refs[-3:]
    block = emb_ref.shape[0]
    table = emb_ref[...]
    local = (ids_ref[...] & (block - 1)).astype(f32)
    sub8 = iota((8, block), 0)
    stack = jnp.zeros((8, block), f32)
    for s in range(p.steps):
        stack = jnp.where(sub8 == s, jnp.broadcast_to(local[s : s + 1, :], (8, block)), stack)
    index = stack.T.astype(jnp.int32)
    logs = jnp.log(tot_ref[...].astype(f32))
    first = logs.astype(bf16).astype(f32)
    second = (logs - first).astype(bf16).astype(f32)
    third = logs - first - second
    sub16 = iota((16, block), 0)
    digits = jnp.where(sub16 == 0, first, jnp.where(sub16 == 1, second, jnp.where(sub16 == 2, third, 0.0)))
    digits = digits.astype(bf16)
    items = iota((block, block), 1)
    out = jnp.zeros((8, block), f32)
    for s in range(p.steps):
        onehot = ones_where(items == index[:, s : s + 1])
        cols_ref[s] = nn(onehot, table).astype(bf16)
        got = nt(digits, onehot)
        row = got[0:1, :] + got[1:2, :] + got[2:3, :]
        out = jnp.where(sub8 == s, jnp.broadcast_to(row, (8, block)), out)
    logs_ref[...] = out

    r, half, mine = position()
    lines = p.steps * p.owners * 8
    group = 128 // p.owners
    slots = p.groups * 4 * p.steps
    hi, lo = split_index(row_ids_ref[...].reshape(lines, 128), p.block)
    lane = iota((128, p.pair), 0)
    inner = iota((128, p.pair), 1) % p.share
    pick = ones_where((lane % p.owners == r) & (lane // p.owners == inner % group))
    keep = iota((lines, p.pair), 0) % 8 == (iota((lines, p.pair), 1) % p.share) // group
    slot = iota((slots, lines), 0)
    line = iota((slots, lines), 1)
    step_ok = line // (p.owners * 8) == slot % p.steps
    q = (slot // p.steps) % 4
    mask = (4 * (slot // (4 * p.steps))) ^ mine ^ turn(q)
    routes = [
        ones_where(step_ok & ((line // 8) % p.owners == (r ^ (2 * mask + (k ^ (q // 2)))))) for k in range(2)
    ]

    def row_of(digit):
        picked = jnp.where(keep, nn(digit, pick), 0.0).astype(bf16)
        return jnp.where(iota((slots, p.pair), 1) < p.share, nn(routes[0], picked), nn(routes[1], picked))

    index_ref[...] = (row_of(hi) * 32.0 + row_of(lo)).astype(jnp.int32)


def columns(p, ids, emb, tot, row_ids, after):
    block, width = emb.shape
    outs = [
        jax.ShapeDtypeStruct((p.steps, block, width), bf16),
        jax.ShapeDtypeStruct((8, block), f32),
        jax.ShapeDtypeStruct((p.groups * 4 * p.steps, p.pair), jnp.int32),
    ]
    args = (ids, emb, tot, row_ids)
    return kernel_call(
        functools.partial(columns_kernel, p), outs, *args, *after, vmem=12,
        in_specs=in_vmem(args) + anywhere(after),
        cost=cost(3),
    )


def pack_kernel(n, a_ref, b_ref, out_ref):
    out_ref[:n, :] = a_ref[n : 2 * n, :]
    out_ref[n : 2 * n, :] = b_ref[n : 2 * n, :]
    if out_ref.shape[0] > 2 * n:
        out_ref[2 * n : 2 * n + 16, :] = a_ref[2 * n :, :]
        out_ref[2 * n + 16 :, :] = b_ref[2 * n :, :]


def pack(a, b):
    rows, width = a.shape
    more = rows % 32
    n = (rows - more) // 2
    return kernel_call(
        functools.partial(pack_kernel, n), jax.ShapeDtypeStruct((2 * n + 2 * more, width), bf16), a, b, vmem=12,
        cost=cost(0),
    )


def factors_kernel(p, scale, step, counts_ref, *refs):
    gain_ref, shift_ref, buf_ref, sems = refs[-4:]
    r, half, mine = position()
    slots = buf_ref.shape[0]
    tiles = counts_ref.shape[2] // 128

    def copy(k):
        src = counts_ref.at[step, :, pl.ds(k * 128, 128)]
        return pltpu.make_async_copy(src, buf_ref.at[k % slots, : p.block], sems.at[k % slots])

    for k in range(slots - 1):
        copy(k).start()
    for k in range(tiles):
        if k + slots - 1 < tiles:
            copy(k + slots - 1).start()
        copy(k).wait()
        for g in range(p.groups):
            for q in range(4):
                for jj in range(2):
                    mask, swapped = fetched(p, g, q, r, mine)
                    owner = r ^ (2 * mask + (jj ^ swapped))
                    x = buf_ref[k % slots, pl.ds(owner, p.share, stride=p.owners), :].astype(f32)
                    safe = jnp.maximum(x, 1.0)
                    root = safe * lax.rsqrt(safe)
                    at = ((g * 4 + q) * 2 + jj) * p.share
                    gain = jnp.where(x > 0.0, (0.1 * scale) + (0.25 * scale) * root, 0.0)
                    gain_ref[at : at + p.share, k * 128 : k * 128 + 128] = gain
                    shift_ref[at : at + p.share, k * 128 : k * 128 + 128] = jnp.log(safe)


def factors(p, scale, counts, step, after, vmem):
    shape = jax.ShapeDtypeStruct(counts.shape[1:], f32)
    slots = 4
    return kernel_call(
        functools.partial(factors_kernel, p, scale, step), [shape, shape], counts, *after, vmem=vmem,
        in_specs=anywhere((counts, *after)), out_specs=in_vmem((shape, shape)),
        scratch_shapes=[
            pltpu.VMEM((slots, p.block + p.owners, 128), jnp.int32),
            pltpu.SemaphoreType.DMA((slots,)),
        ],
        cost=cost(0),
    )


def grads_kernel(p, scale, g, steps, done, has_acc, *refs):
    n = len(steps)
    size = p.steps * p.pair
    m = 3 if g else 4
    msgs, refs = refs[:m], refs[m:]
    if g:
        here, there, crossed = msgs
        sources = [(here, 0, 2 * size), (there, 0, 2 * size), (crossed, 0, 2 * size), (crossed, size, 2 * size + 16)]
    else:
        sources = [(msg, 0, size) for msg in msgs]
    cols_ref, col_logs_ref = refs[:2]
    factor_refs = refs[2 : 2 + 2 * n]
    outs, acc_refs, rows_ref = refs[-4 - n : -1 - n], refs[-1 - n : -1], refs[-1]
    befores = refs[2 + 2 * n : 2 + 3 * n]
    total = (done + n) * p.pair
    if done:
        old = done * p.pair
        prior = refs[2 + (3 if has_acc else 2) * n :][:3]
        outs[0][:old, :] = prior[0][...]
        outs[1][:old, :] = prior[1][...]
        outs[2][:old, :] = prior[2][:old, :]
        outs[2][total : total + old, :] = prior[2][old:, :]
    r, half, mine = position()
    targets = [(outs[0], 0), (outs[2], 0), (outs[1], 0), (outs[2], total)]
    group = max(1, 256 // p.pair)
    for i, s in enumerate(steps):
        cols = cols_ref[s]
        col_logs = col_logs_ref[s : s + 1, :] - log_total
        for q0 in range(0, 4, group):
            members = range(q0, min(q0 + group, 4))
            pieces, row_logs = [], []
            for q in members:
                msg, lo, end = sources[q]
                lo += s * p.pair
                pieces.append(msg[lo : lo + p.pair, :])
                logs = msg[end : end + 16, :128].astype(f32).T
                e = 2 * (g + 1) + q // 2 if g else q
                off = (e * p.share) % 128
                for jj in range(2):
                    row_logs.append(logs[off : off + p.share, s * 2 + jj : s * 2 + jj + 1])
            x = jnp.concatenate(pieces, axis=0)
            rows = x.shape[0]
            z = nt(x, cols) + (jnp.concatenate(row_logs, axis=0) + col_logs)
            at = (4 * g + q0) * p.pair
            gain = factor_refs[2 * i][at : at + rows, :]
            fitted = gain * (z - factor_refs[2 * i + 1][at : at + rows, :])
            hinge = (0.5 * scale) * jnp.tanh(0.5 * z) + (0.5 * scale)
            weights = jnp.where(gain > 0.0, fitted, hinge).astype(bf16)
            got = nn(weights, cols)
            if g:
                for k, q in enumerate(members):
                    out, lo = targets[q]
                    lo += (done + i) * p.pair
                    out[lo : lo + p.pair, :] = got[k * p.pair : (k + 1) * p.pair].astype(out.dtype)
            else:
                rows_ref[q0 * p.pair : q0 * p.pair + rows, :] = got
            c = tn(x, weights)
            if q0 == 0:
                acc_refs[i][...] = befores[i][...] + c if has_acc else c
            else:
                acc_refs[i][...] += c
        if not g:
            for q, (out, lo) in enumerate(targets):
                mask = mine ^ turn(q)
                for k in range(2):
                    at = pl.multiple_of(mask * p.pair + (k ^ (q // 2)) * p.share, p.share)
                    to = lo + (done + i) * p.pair + k * p.share
                    out[to : to + p.share, :] = rows_ref[pl.ds(at, p.share), :].astype(out.dtype)


def grads(p, scale, g, steps, msgs, cols, col_logs, factor, acc=(), prior=()):
    block = cols.shape[1]
    done = prior[0].shape[0] // p.pair if prior else 0
    n = (done + len(steps)) * p.pair
    stay = jax.ShapeDtypeStruct((n, p.width), f32)
    outs = [stay, stay, jax.ShapeDtypeStruct((2 * n, p.width), bf16)]
    outs += [jax.ShapeDtypeStruct((p.width, block), f32)] * len(steps)
    args = (*msgs, cols, col_logs, *factor, *acc, *prior)
    return kernel_call(
        functools.partial(grads_kernel, p, scale, g, steps, done, bool(acc)), outs, *args, vmem=14,
        scratch_shapes=[pltpu.VMEM((4 * p.pair, p.width), f32)],
        cost=cost(0),
    )


def meet_kernel(own_ref, pass_ref, got_ref, *refs):
    own_out, pass_out = refs[-2:]
    n = own_ref.shape[0]
    own_out[...] = (own_ref[...] + got_ref[:n, :].astype(f32)).astype(bf16)
    pass_out[...] = (pass_ref[...] + got_ref[n:, :].astype(f32)).astype(bf16)


def meet(own, passed, got, after):
    outs = [jax.ShapeDtypeStruct(own.shape, bf16)] * 2
    args = (own, passed, got)
    return kernel_call(
        meet_kernel, outs, *args, *after, vmem=12, in_specs=in_vmem(args) + anywhere(after), cost=cost(0)
    )


def merge_kernel(p, own_ref, core_ref, *refs):
    out = refs[-1]
    n = own_ref.shape[0]
    for d in range(2):
        for at in range(0, n, p.pair):
            src = slice(at + d * p.share, at + (d + 1) * p.share)
            lo = d * n + at
            out[lo : lo + p.share, :] = own_ref[src, :]
            out[lo + p.share : lo + p.pair, :] = core_ref[src, :]


def merge(p, own, core, after=()):
    args = (own, core)
    return kernel_call(
        functools.partial(merge_kernel, p),
        jax.ShapeDtypeStruct((2 * own.shape[0], p.width), bf16), *args, *after,
        vmem=12, in_specs=in_vmem(args) + anywhere(after), cost=cost(0),
    )


def collect_kernel(p, first, steps, has_acc, index_ref, *refs):
    msgs, out_ref = refs[:2], refs[-1]
    bases = (0, first % 4 // 2)
    items = iota((p.block, p.pair), 0)
    total = refs[2][...] if has_acc else None
    for i, s in enumerate(steps):
        at = [(first + k) * p.steps + s for k in range(2)]
        onehot = jnp.concatenate([ones_where(items == index_ref[k : k + 1, :]) for k in at], axis=1)
        lo = [(base * len(steps) + i) * p.pair for base in bases]
        rows = jnp.concatenate([m[k : k + p.pair, :] for m, k in zip(msgs, lo)], axis=0)
        term = nn(onehot, rows)
        total = term if total is None else total + term
    out_ref[...] = total


def collect(p, first, steps, index, msgs, acc=None):
    args = (index, *msgs) + (() if acc is None else (acc,))
    return kernel_call(
        functools.partial(collect_kernel, p, first, steps, acc is not None),
        jax.ShapeDtypeStruct((p.block, p.width), f32), *args, vmem=12,
        cost=cost(1),
    )


def finish_kernel(p, first, steps, index_ref, a_ref, b_ref, acc_ref, mine_ref, other_ref, rows_ref, cols_ref):
    half = mine_ref.shape[0]
    core = lax.axis_index("row") % 2
    cols_ref[pl.ds(pl.multiple_of(core * half, half), half), :] = mine_ref[...].astype(f32)
    cols_ref[pl.ds(pl.multiple_of((1 - core) * half, half), half), :] = other_ref[...].astype(f32)
    collect_kernel(p, first, steps, True, index_ref, a_ref, b_ref, acc_ref, rows_ref)


def finish(p, first, steps, index, msgs, acc, mine, other):
    outs = [
        jax.ShapeDtypeStruct((p.block, p.width), f32),
        jax.ShapeDtypeStruct((2 * mine.shape[0], p.width), f32),
    ]
    return kernel_call(
        functools.partial(finish_kernel, p, first, steps), outs, index, *msgs, acc, mine, other, vmem=16,
        cost=cost(0),
    )


def place_kernel(step, final, ids_ref, sum_ref, *refs):
    r = lax.axis_index("row")
    block = sum_ref.shape[1]
    local = ids_ref[...] & (block - 1)
    items = iota((block, block), 0)
    total = sum_ref[...]
    top = total.astype(bf16)
    rest = (total - top.astype(f32)).astype(bf16)
    onehot = ones_where(items == local[step : step + 1, :])
    term = nt(onehot, top) + nt(onehot, rest)
    if step:
        term = term + refs[0][...]
    if not final:
        refs[-1][...] = term
        return
    mine_ref, top_ref, rest_ref, acc_ref = refs[-4:]
    acc_ref[...] = term
    part = block // 2
    mine_ref[...] = acc_ref[pl.ds(pl.multiple_of((r % 2) * part, part), part), :]
    other = acc_ref[pl.ds(pl.multiple_of((1 - r % 2) * part, part), part), :]
    top_ref[...] = other.astype(bf16)
    rest_ref[...] = (other - other.astype(bf16).astype(f32)).astype(bf16)


def place(step, final, ids, sums, acc=(), after=()):
    width, block = sums.shape
    if final:
        outs = [jax.ShapeDtypeStruct((block // 2, width), kind) for kind in (f32, bf16, bf16)]
        scratch = [pltpu.VMEM((block, width), f32)]
    else:
        outs = [jax.ShapeDtypeStruct((block, width), f32)]
        scratch = []
    return kernel_call(
        functools.partial(place_kernel, step, final), outs, ids, sums, *acc, *after, vmem=12,
        in_specs=in_vmem((ids, sums, *acc)) + anywhere(after),
        scratch_shapes=scratch,
        cost=cost(0),
    )


def spread_kernel(parts, stride, count, after, *refs):
    mine, arrived = refs[0], refs[1 : 1 + count]
    outs, acc_ref = refs[1 + count + after : -1], refs[-1]
    here = (lax.axis_index("row") // stride) % parts
    total = mine[...]
    for a in arrived:
        total = total + a[...].astype(f32)
    acc_ref[...] = total
    size = outs[0].shape[0]
    for k, out in enumerate(outs):
        at = pl.multiple_of((here ^ k) * size, size)
        out[...] = acc_ref[pl.ds(at, size), :].astype(out.dtype)


def spread(parts, stride, mine, arrived, after=()):
    rows, width = mine.shape
    size = rows // parts
    outs = [jax.ShapeDtypeStruct((size, width), bf16 if (parts == 1 or k) else f32) for k in range(parts)]
    return kernel_call(
        functools.partial(spread_kernel, parts, stride, len(arrived), len(after)), outs, mine, *arrived, *after,
        vmem=16, in_specs=in_vmem((mine, *arrived)) + anywhere(after),
        scratch_shapes=[pltpu.VMEM((rows, width), f32)],
        cost=cost(0),
    )


def add_kernel(a_ref, b_ref, out_ref):
    out_ref[...] = (a_ref[...].astype(f32) + b_ref[...].astype(f32)).astype(out_ref.dtype)


def add(a, b):
    return kernel_call(add_kernel, jax.ShapeDtypeStruct(a.shape, a.dtype), a, b, vmem=12, cost=cost(0))


def gather_kernel(parts, stride, *refs):
    pieces, out = refs[:-1], refs[-1]
    here = (lax.axis_index("row") // stride) % parts
    size = pieces[0].shape[0]
    for k, piece in enumerate(pieces):
        at = pl.multiple_of((here ^ k) * size, size)
        value = piece[...].astype(out.dtype)
        out[pl.ds(at, size), :] = value


def gather(stride, pieces, dtype=bf16):
    parts = len(pieces)
    rows, width = pieces[0].shape
    return kernel_call(
        functools.partial(gather_kernel, parts, stride),
        jax.ShapeDtypeStruct((parts * rows, width), dtype), *pieces, vmem=16,
        cost=cost(0),
    )


def local(row_emb, col_emb, counts, row_totals, col_totals, row_ids, col_ids):
    owners = lax.axis_size("row")
    cols_n = lax.axis_size("col")
    block, width = row_emb.shape
    block_cols = col_emb.shape[0]
    steps = counts.shape[0]
    p = Plan(owners, steps, block, width)
    scale = (steps * math.sqrt(owners * block * cols_n * block_cols)) ** (-0.5)

    def row_swap(x, mask):
        return lax.ppermute(x, "row", [(i, i ^ mask) for i in range(owners)])

    def col_swap(x, mask=1):
        return lax.ppermute(x, "col", [(i, i ^ mask) for i in range(cols_n)])

    def grid_swap(x, mask_of):
        perm = []
        for i in range(owners):
            for j in range(cols_n):
                row_mask, col_mask = mask_of(2 * (i % 2) + j % 2)
                perm.append((i * cols_n + j, (i ^ row_mask) * cols_n + (j ^ col_mask)))
        return lax.ppermute(x, ("row", "col"), perm)

    def tie(x, *others):
        return lax.optimization_barrier((x, *others))[0]

    def carry(x, group):
        return grid_swap(x, lambda t: (2 * ((4 * group) ^ turn(t)), 0))

    ids = row_ids.reshape(steps, owners * block // 128, 128)
    totals = row_totals.reshape(1, block)
    msgs = fetch(p, ids, row_emb, row_swap(row_emb, 1), totals, row_swap(totals, 1))
    far = [carry(msgs[3 + g], g) for g in range(1, p.groups)]
    near = [msgs[0]] + [row_swap(msgs[k], 2 * k) for k in range(1, 4)]
    cols, col_logs, index = columns(
        p, col_ids, col_emb, col_totals.reshape(1, block_cols), ids, (msgs[0],)
    )

    every = tuple(range(steps))
    factor = []
    last = (col_logs,)
    term = ()
    sums = []
    for s in every:
        factor += factors(p, scale, counts, s, last, 44 if s == 0 else 38)
        if s == 0:
            *term, total = grads(p, scale, 0, (s,), near, cols, col_logs, factor)
            sums.append(total)
        last = (factor[-1],)
        if s == 0:
            far = [tie(x, *(sums or last), *near[1:]) for x in far]
            last = (*last, *far)
    near[1] = tie(near[1], *last)
    rest = every[len(sums) :]
    term = grads(p, scale, 0, rest, near, cols, col_logs, factor[2 * len(sums) :], (), tuple(term))
    sums += term[3:]
    terms = [term[:3]]
    acc0 = sums[-1]
    crossed = []
    for g in range(1, p.groups):
        here = far[g - 1]
        there = tie(col_swap(here), acc0)
        crossed.append(there)
        four = (here, there, row_swap(pack(here, there), 1))
        made = grads(p, scale, g, every, four, cols, col_logs, factor, tuple(sums))
        terms.append(made[:3])
        sums = made[3:]

    met = [col_swap(t[2] if g else tie(t[2], *crossed)) for g, t in enumerate(terms)]
    placed = ()
    for s in every:
        placed = place(s, s + 1 == steps, col_ids, sums[s], placed)
    mine, *parts = placed
    mine, *others = spread(p.wide, 2, mine, [row_swap(x, 1) for x in parts])
    parcels = []
    for g, (own, passed, _) in enumerate(terms):
        own, passed = meet(own, passed, met[g], () if g else placed[:1])
        parcels.append(merge(p, own, row_swap(passed, 1)))
    (piece,) = spread(1, 1, mine, [row_swap(x, (k + 1) * 2) for k, x in enumerate(others)])
    heres = [carry(x, g) for g, x in enumerate(parcels)]
    theres = [col_swap(x) for x in heres]

    stride = 2 * p.wide
    while stride < owners:
        piece = add(piece, row_swap(piece, stride))
        stride *= 2
    piece = gather(2, [piece] + [row_swap(piece, k * 2) for k in range(1, p.wide)])

    rows = None
    for g, (here, there) in enumerate(zip(heres, theres)):
        rows = collect(p, 4 * g, every, index, (here, there), rows)
        other = row_swap(pack(here, there), 1)
        if g + 1 < p.groups:
            rows = collect(p, 4 * g + 2, every, index, (other, other), rows)
    last = 4 * p.groups - 2
    rows, grad_cols = finish(p, last, every, index, (other, other), rows, piece, row_swap(piece, 1))

    if cols_n > 2:
        total = rows
        for mask in range(2, cols_n, 2):
            total = total + col_swap(rows.astype(bf16), mask).astype(f32)
        rows = total
    return rows, grad_cols


def solution(mesh):
    in_specs = (
        P("row", None),
        P("col", None),
        P(None, "row", "col"),
        P("row"),
        P("col"),
        P(),
        P(None, "col"),
    )
    out_specs = (P("row", None), P("col", None))
    return jax.shard_map(local, mesh=mesh, in_specs=in_specs, out_specs=out_specs, check_vma=False)
```

```python
import functools
import math

import jax
import jax.numpy as jnp
from jax import lax
from jax.experimental import pallas as pl
from jax.experimental.pallas import tpu as pltpu
from jax.sharding import PartitionSpec as P

log_total = 8.0
f32 = jnp.float32
bf16 = jnp.bfloat16
MIB = 1 << 20


def nt(a, b):
    return lax.dot_general(a, b, (((1,), (1,)), ((), ())), preferred_element_type=f32)


def tn(a, b):
    return lax.dot_general(a, b, (((0,), (0,)), ((), ())), preferred_element_type=f32)


def nn(a, b):
    return jnp.dot(a, b, preferred_element_type=f32)


def iota(shape, dim):
    return lax.broadcasted_iota(jnp.int32, shape, dim)


def ones_where(cond):
    return jnp.where(cond, 1.0, 0.0).astype(bf16)


def split_index(ids, size):
    local = ids & (size - 1)
    return (local >> 5).astype(f32).astype(bf16), (local & 31).astype(f32).astype(bf16)


def kernel_call(body, outs, *args, vmem=32, cost=None, **kw):
    return pl.pallas_call(
        body,
        out_shape=outs,
        compiler_params=pltpu.CompilerParams(vmem_limit_bytes=vmem * MIB),
        cost_estimate=cost,
        **kw,
    )(*args)


def cost(us):
    return pl.CostEstimate(flops=int(us * 1.1e9), bytes_accessed=1, transcendentals=0)


def anywhere(items):
    return [pl.BlockSpec(memory_space=pl.ANY)] * len(items)


def in_vmem(items):
    return [pl.BlockSpec(memory_space=pltpu.VMEM)] * len(items)


class Plan:
    def __init__(self, owners, steps, block, width):
        self.owners = owners
        self.steps = steps
        self.block = block
        self.width = width
        self.chips = owners // 2
        self.groups = self.chips // 4
        self.share = block // owners
        self.pair = 2 * self.share
        self.deep = min(4, self.chips)
        self.wide = self.chips // self.deep
        self.slots = 2 * self.groups + 2


def turn(t):
    return ((t & 1) * 2) ^ ((t >> 1) * 3)


def position():
    r = lax.axis_index("row")
    half = lax.axis_index("col") % 2
    return r, half, turn(2 * (r % 2) + half)


def fetched(p, g, q, r, mine):
    if g:
        return (4 * g) ^ turn(q) ^ mine, q // 2
    return q, 0


def fetch_kernel(p, ids_ref, own_ref, oth_ref, tot_own_ref, tot_oth_ref, *msgs):
    r, half, mine = position()
    lines = p.steps * p.owners * 8
    group = 128 // p.owners
    count = p.slots
    hi, lo = split_index(ids_ref[...].reshape(lines, 128), p.block)
    sub = iota((p.pair, 128), 0)
    lane = iota((p.pair, 128), 1)
    owner = r ^ (sub // p.share)
    inner = sub % p.share
    pick = ones_where((lane % p.owners == owner) & (lane // p.owners == inner % group))
    sub2 = iota((p.pair, lines), 0) % p.share
    lane2 = iota((p.pair, lines), 1)
    keep = lane2 % 8 == sub2 // group
    line = iota((lines, 128), 0)
    slot = iota((lines, 128), 1)
    step_ok = line // (p.owners * 8) == slot // count
    dest = (line // 8) % p.owners
    e = slot % count
    far = 2 * ((4 * (e // 2 - 1)) ^ mine) + e % 2
    route = ones_where(step_ok & (dest == (r ^ jnp.where(e < 4, 2 * e, far))))

    def column(digit):
        picked = jnp.where(keep, nt(pick, digit), 0.0).astype(bf16)
        return nn(picked, route)

    index = (column(hi) * 32.0 + column(lo)).astype(jnp.int32)
    logs = jnp.zeros((16, count * p.share), f32)
    log_row = iota((16, count * p.share), 0)
    items = iota((p.share, p.block), 1)
    tables = [own_ref, oth_ref]
    totals = [tot_own_ref, tot_oth_ref]
    for jj in range(2):
        table_log = jnp.log(totals[jj][...].astype(f32)).astype(bf16)
        table_log = jnp.broadcast_to(table_log, (16, p.block))
        for s in range(p.steps):
            pieces = []
            for e in range(count):
                n = s * count + e
                col = index[jj * p.share : (jj + 1) * p.share, n : n + 1]
                pieces.append(ones_where(items == col))
            onehot = jnp.concatenate(pieces, axis=0)
            rows = nn(onehot, tables[jj][...]).astype(bf16)
            logs = logs + jnp.where(log_row == s * 2 + jj, nt(table_log, onehot), 0.0)
            for e in range(count):
                piece = rows[e * p.share : (e + 1) * p.share, :]
                if e < 4:
                    msg, at = msgs[e], s * p.pair
                else:
                    msg, at = msgs[2 + e // 2], (e % 2 * p.steps + s) * p.pair
                msg[at + jj * p.share : at + (jj + 1) * p.share, :] = piece
    for k, msg in enumerate(msgs):
        e = k if k < 4 else 2 * k - 4
        tile = (e * p.share) // 128 * 128
        end = msg.shape[0] - 16
        wide = min(128, count * p.share - tile)
        msg[end : end + 16, :] = jnp.zeros((16, p.width), bf16)
        msg[end : end + 16, :wide] = logs[:, tile : tile + wide].astype(bf16)


def fetch(p, ids, own, oth, tot_own, tot_oth):
    n = p.steps * p.pair
    outs = [jax.ShapeDtypeStruct((k * n + 16, p.width), bf16) for k in [1] * 4 + [2] * (p.groups - 1)]
    return kernel_call(
        functools.partial(fetch_kernel, p), outs, ids, own, oth, tot_own, tot_oth, vmem=12,
        cost=cost(3),
    )


def columns_kernel(p, ids_ref, emb_ref, tot_ref, row_ids_ref, *refs):
    cols_ref, logs_ref, index_ref = refs[-3:]
    block = emb_ref.shape[0]
    table = emb_ref[...]
    local = (ids_ref[...] & (block - 1)).astype(f32)
    sub8 = iota((8, block), 0)
    stack = jnp.zeros((8, block), f32)
    for s in range(p.steps):
        stack = jnp.where(sub8 == s, jnp.broadcast_to(local[s : s + 1, :], (8, block)), stack)
    index = stack.T.astype(jnp.int32)
    logs = jnp.log(tot_ref[...].astype(f32))
    first = logs.astype(bf16).astype(f32)
    second = (logs - first).astype(bf16).astype(f32)
    third = logs - first - second
    sub16 = iota((16, block), 0)
    digits = jnp.where(sub16 == 0, first, jnp.where(sub16 == 1, second, jnp.where(sub16 == 2, third, 0.0)))
    digits = digits.astype(bf16)
    items = iota((block, block), 1)
    out = jnp.zeros((8, block), f32)
    for s in range(p.steps):
        onehot = ones_where(items == index[:, s : s + 1])
        cols_ref[s] = nn(onehot, table).astype(bf16)
        got = nt(digits, onehot)
        row = got[0:1, :] + got[1:2, :] + got[2:3, :]
        out = jnp.where(sub8 == s, jnp.broadcast_to(row, (8, block)), out)
    logs_ref[...] = out

    r, half, mine = position()
    lines = p.steps * p.owners * 8
    group = 128 // p.owners
    slots = p.groups * 4 * p.steps
    hi, lo = split_index(row_ids_ref[...].reshape(lines, 128), p.block)
    lane = iota((128, p.pair), 0)
    inner = iota((128, p.pair), 1) % p.share
    pick = ones_where((lane % p.owners == r) & (lane // p.owners == inner % group))
    keep = iota((lines, p.pair), 0) % 8 == (iota((lines, p.pair), 1) % p.share) // group
    slot = iota((slots, lines), 0)
    line = iota((slots, lines), 1)
    step_ok = line // (p.owners * 8) == slot % p.steps
    q = (slot // p.steps) % 4
    mask = (4 * (slot // (4 * p.steps))) ^ mine ^ turn(q)
    routes = [
        ones_where(step_ok & ((line // 8) % p.owners == (r ^ (2 * mask + (k ^ (q // 2)))))) for k in range(2)
    ]

    def row_of(digit):
        picked = jnp.where(keep, nn(digit, pick), 0.0).astype(bf16)
        return jnp.where(iota((slots, p.pair), 1) < p.share, nn(routes[0], picked), nn(routes[1], picked))

    index_ref[...] = (row_of(hi) * 32.0 + row_of(lo)).astype(jnp.int32)


def columns(p, ids, emb, tot, row_ids, after):
    block, width = emb.shape
    outs = [
        jax.ShapeDtypeStruct((p.steps, block, width), bf16),
        jax.ShapeDtypeStruct((8, block), f32),
        jax.ShapeDtypeStruct((p.groups * 4 * p.steps, p.pair), jnp.int32),
    ]
    args = (ids, emb, tot, row_ids)
    return kernel_call(
        functools.partial(columns_kernel, p), outs, *args, *after, vmem=12,
        in_specs=in_vmem(args) + anywhere(after),
        cost=cost(3),
    )


def pack_kernel(n, a_ref, b_ref, out_ref):
    out_ref[:n, :] = a_ref[n : 2 * n, :]
    out_ref[n : 2 * n, :] = b_ref[n : 2 * n, :]
    if out_ref.shape[0] > 2 * n:
        out_ref[2 * n : 2 * n + 16, :] = a_ref[2 * n :, :]
        out_ref[2 * n + 16 :, :] = b_ref[2 * n :, :]


def pack(a, b):
    rows, width = a.shape
    more = rows % 32
    n = (rows - more) // 2
    return kernel_call(
        functools.partial(pack_kernel, n), jax.ShapeDtypeStruct((2 * n + 2 * more, width), bf16), a, b, vmem=12,
        cost=cost(0),
    )


def factors_kernel(p, scale, step, counts_ref, *refs):
    gain_ref, shift_ref, buf_ref, sems = refs[-4:]
    r, half, mine = position()
    slots = buf_ref.shape[0]
    tiles = counts_ref.shape[2] // 128

    def copy(k):
        src = counts_ref.at[step, :, pl.ds(k * 128, 128)]
        return pltpu.make_async_copy(src, buf_ref.at[k % slots, : p.block], sems.at[k % slots])

    for k in range(slots - 1):
        copy(k).start()
    for k in range(tiles):
        if k + slots - 1 < tiles:
            copy(k + slots - 1).start()
        copy(k).wait()
        for g in range(p.groups):
            for q in range(4):
                for jj in range(2):
                    mask, swapped = fetched(p, g, q, r, mine)
                    owner = r ^ (2 * mask + (jj ^ swapped))
                    x = buf_ref[k % slots, pl.ds(owner, p.share, stride=p.owners), :].astype(f32)
                    safe = jnp.maximum(x, 1.0)
                    root = safe * lax.rsqrt(safe)
                    at = ((g * 4 + q) * 2 + jj) * p.share
                    gain = jnp.where(x > 0.0, (0.1 * scale) + (0.25 * scale) * root, 0.0)
                    gain_ref[at : at + p.share, k * 128 : k * 128 + 128] = gain
                    shift_ref[at : at + p.share, k * 128 : k * 128 + 128] = jnp.log(safe)


def factors(p, scale, counts, step, after, vmem):
    shape = jax.ShapeDtypeStruct(counts.shape[1:], f32)
    slots = 4
    return kernel_call(
        functools.partial(factors_kernel, p, scale, step), [shape, shape], counts, *after, vmem=vmem,
        in_specs=anywhere((counts, *after)), out_specs=in_vmem((shape, shape)),
        scratch_shapes=[
            pltpu.VMEM((slots, p.block + p.owners, 128), jnp.int32),
            pltpu.SemaphoreType.DMA((slots,)),
        ],
        cost=cost(0),
    )


def grads_kernel(p, scale, g, steps, done, has_acc, *refs):
    n = len(steps)
    size = p.steps * p.pair
    m = 3 if g else 4
    msgs, refs = refs[:m], refs[m:]
    if g:
        here, there, crossed = msgs
        sources = [(here, 0, 2 * size), (there, 0, 2 * size), (crossed, 0, 2 * size), (crossed, size, 2 * size + 16)]
    else:
        sources = [(msg, 0, size) for msg in msgs]
    cols_ref, col_logs_ref = refs[:2]
    factor_refs = refs[2 : 2 + 2 * n]
    outs, acc_refs, rows_ref = refs[-4 - n : -1 - n], refs[-1 - n : -1], refs[-1]
    befores = refs[2 + 2 * n : 2 + 3 * n]
    total = (done + n) * p.pair
    if done:
        old = done * p.pair
        prior = refs[2 + (3 if has_acc else 2) * n :][:3]
        outs[0][:old, :] = prior[0][...]
        outs[1][:old, :] = prior[1][...]
        outs[2][:old, :] = prior[2][:old, :]
        outs[2][total : total + old, :] = prior[2][old:, :]
    r, half, mine = position()
    targets = [(outs[0], 0), (outs[2], 0), (outs[1], 0), (outs[2], total)]
    group = max(1, 256 // p.pair)
    for i, s in enumerate(steps):
        cols = cols_ref[s]
        col_logs = col_logs_ref[s : s + 1, :] - log_total
        for q0 in range(0, 4, group):
            members = range(q0, min(q0 + group, 4))
            pieces, row_logs = [], []
            for q in members:
                msg, lo, end = sources[q]
                lo += s * p.pair
                pieces.append(msg[lo : lo + p.pair, :])
                logs = msg[end : end + 16, :128].astype(f32).T
                e = 2 * (g + 1) + q // 2 if g else q
                off = (e * p.share) % 128
                for jj in range(2):
                    row_logs.append(logs[off : off + p.share, s * 2 + jj : s * 2 + jj + 1])
            x = jnp.concatenate(pieces, axis=0)
            rows = x.shape[0]
            z = nt(x, cols) + (jnp.concatenate(row_logs, axis=0) + col_logs)
            at = (4 * g + q0) * p.pair
            gain = factor_refs[2 * i][at : at + rows, :]
            fitted = gain * (z - factor_refs[2 * i + 1][at : at + rows, :])
            hinge = (0.5 * scale) * jnp.tanh(0.5 * z) + (0.5 * scale)
            weights = jnp.where(gain > 0.0, fitted, hinge).astype(bf16)
            got = nn(weights, cols)
            if g:
                for k, q in enumerate(members):
                    out, lo = targets[q]
                    lo += (done + i) * p.pair
                    out[lo : lo + p.pair, :] = got[k * p.pair : (k + 1) * p.pair].astype(out.dtype)
            else:
                rows_ref[q0 * p.pair : q0 * p.pair + rows, :] = got
            c = tn(x, weights)
            if q0 == 0:
                acc_refs[i][...] = befores[i][...] + c if has_acc else c
            else:
                acc_refs[i][...] += c
        if not g:
            for q, (out, lo) in enumerate(targets):
                mask = mine ^ turn(q)
                for k in range(2):
                    at = pl.multiple_of(mask * p.pair + (k ^ (q // 2)) * p.share, p.share)
                    to = lo + (done + i) * p.pair + k * p.share
                    out[to : to + p.share, :] = rows_ref[pl.ds(at, p.share), :].astype(out.dtype)


def grads(p, scale, g, steps, msgs, cols, col_logs, factor, acc=(), prior=()):
    block = cols.shape[1]
    done = prior[0].shape[0] // p.pair if prior else 0
    n = (done + len(steps)) * p.pair
    stay = jax.ShapeDtypeStruct((n, p.width), f32)
    outs = [stay, stay, jax.ShapeDtypeStruct((2 * n, p.width), bf16)]
    outs += [jax.ShapeDtypeStruct((p.width, block), f32)] * len(steps)
    args = (*msgs, cols, col_logs, *factor, *acc, *prior)
    return kernel_call(
        functools.partial(grads_kernel, p, scale, g, steps, done, bool(acc)), outs, *args, vmem=14,
        scratch_shapes=[pltpu.VMEM((4 * p.pair, p.width), f32)],
        cost=cost(0),
    )


def meet_kernel(own_ref, pass_ref, got_ref, *refs):
    own_out, pass_out = refs[-2:]
    n = own_ref.shape[0]
    own_out[...] = (own_ref[...] + got_ref[:n, :].astype(f32)).astype(bf16)
    pass_out[...] = (pass_ref[...] + got_ref[n:, :].astype(f32)).astype(bf16)


def meet(own, passed, got, after):
    outs = [jax.ShapeDtypeStruct(own.shape, bf16)] * 2
    args = (own, passed, got)
    return kernel_call(
        meet_kernel, outs, *args, *after, vmem=12, in_specs=in_vmem(args) + anywhere(after), cost=cost(0)
    )


def merge_kernel(p, own_ref, core_ref, *refs):
    out = refs[-1]
    n = own_ref.shape[0]
    for d in range(2):
        for at in range(0, n, p.pair):
            src = slice(at + d * p.share, at + (d + 1) * p.share)
            lo = d * n + at
            out[lo : lo + p.share, :] = own_ref[src, :]
            out[lo + p.share : lo + p.pair, :] = core_ref[src, :]


def merge(p, own, core, after=()):
    args = (own, core)
    return kernel_call(
        functools.partial(merge_kernel, p),
        jax.ShapeDtypeStruct((2 * own.shape[0], p.width), bf16), *args, *after,
        vmem=12, in_specs=in_vmem(args) + anywhere(after), cost=cost(0),
    )


def collect_kernel(p, first, steps, has_acc, index_ref, *refs):
    msgs, out_ref = refs[:2], refs[-1]
    bases = (0, first % 4 // 2)
    items = iota((p.block, p.pair), 0)
    total = refs[2][...] if has_acc else None
    for i, s in enumerate(steps):
        at = [(first + k) * p.steps + s for k in range(2)]
        onehot = jnp.concatenate([ones_where(items == index_ref[k : k + 1, :]) for k in at], axis=1)
        lo = [(base * len(steps) + i) * p.pair for base in bases]
        rows = jnp.concatenate([m[k : k + p.pair, :] for m, k in zip(msgs, lo)], axis=0)
        term = nn(onehot, rows)
        total = term if total is None else total + term
    out_ref[...] = total


def collect(p, first, steps, index, msgs, acc=None):
    args = (index, *msgs) + (() if acc is None else (acc,))
    return kernel_call(
        functools.partial(collect_kernel, p, first, steps, acc is not None),
        jax.ShapeDtypeStruct((p.block, p.width), f32), *args, vmem=12,
        cost=cost(1),
    )


def finish_kernel(p, first, steps, index_ref, a_ref, b_ref, acc_ref, mine_ref, other_ref, rows_ref, cols_ref):
    half = mine_ref.shape[0]
    core = lax.axis_index("row") % 2
    cols_ref[pl.ds(pl.multiple_of(core * half, half), half), :] = mine_ref[...].astype(f32)
    cols_ref[pl.ds(pl.multiple_of((1 - core) * half, half), half), :] = other_ref[...].astype(f32)
    collect_kernel(p, first, steps, True, index_ref, a_ref, b_ref, acc_ref, rows_ref)


def finish(p, first, steps, index, msgs, acc, mine, other):
    outs = [
        jax.ShapeDtypeStruct((p.block, p.width), f32),
        jax.ShapeDtypeStruct((2 * mine.shape[0], p.width), f32),
    ]
    return kernel_call(
        functools.partial(finish_kernel, p, first, steps), outs, index, *msgs, acc, mine, other, vmem=16,
        cost=cost(0),
    )


def place_kernel(step, final, ids_ref, sum_ref, *refs):
    r = lax.axis_index("row")
    block = sum_ref.shape[1]
    local = ids_ref[...] & (block - 1)
    items = iota((block, block), 0)
    total = sum_ref[...]
    top = total.astype(bf16)
    rest = (total - top.astype(f32)).astype(bf16)
    onehot = ones_where(items == local[step : step + 1, :])
    term = nt(onehot, top) + nt(onehot, rest)
    if step:
        term = term + refs[0][...]
    if not final:
        refs[-1][...] = term
        return
    mine_ref, other_ref, acc_ref = refs[-3:]
    acc_ref[...] = term
    part = block // 2
    mine_ref[...] = acc_ref[pl.ds(pl.multiple_of((r % 2) * part, part), part), :]
    other = acc_ref[pl.ds(pl.multiple_of((1 - r % 2) * part, part), part), :]
    other_ref[...] = other.astype(bf16)


def place(step, final, ids, sums, acc=(), after=()):
    width, block = sums.shape
    if final:
        outs = [jax.ShapeDtypeStruct((block // 2, width), kind) for kind in (f32, bf16)]
        scratch = [pltpu.VMEM((block, width), f32)]
    else:
        outs = [jax.ShapeDtypeStruct((block, width), f32)]
        scratch = []
    return kernel_call(
        functools.partial(place_kernel, step, final), outs, ids, sums, *acc, *after, vmem=12,
        in_specs=in_vmem((ids, sums, *acc)) + anywhere(after),
        scratch_shapes=scratch,
        cost=cost(0),
    )


def spread_kernel(parts, stride, count, after, *refs):
    mine, arrived = refs[0], refs[1 : 1 + count]
    outs, acc_ref = refs[1 + count + after : -1], refs[-1]
    here = (lax.axis_index("row") // stride) % parts
    total = mine[...]
    for a in arrived:
        total = total + a[...].astype(f32)
    acc_ref[...] = total
    size = outs[0].shape[0]
    for k, out in enumerate(outs):
        at = pl.multiple_of((here ^ k) * size, size)
        out[...] = acc_ref[pl.ds(at, size), :].astype(out.dtype)


def spread(parts, stride, mine, arrived, after=()):
    rows, width = mine.shape
    size = rows // parts
    outs = [jax.ShapeDtypeStruct((size, width), bf16 if (parts == 1 or k) else f32) for k in range(parts)]
    return kernel_call(
        functools.partial(spread_kernel, parts, stride, len(arrived), len(after)), outs, mine, *arrived, *after,
        vmem=16, in_specs=in_vmem((mine, *arrived)) + anywhere(after),
        scratch_shapes=[pltpu.VMEM((rows, width), f32)],
        cost=cost(0),
    )


def add_kernel(a_ref, b_ref, out_ref):
    out_ref[...] = (a_ref[...].astype(f32) + b_ref[...].astype(f32)).astype(out_ref.dtype)


def add(a, b):
    return kernel_call(add_kernel, jax.ShapeDtypeStruct(a.shape, a.dtype), a, b, vmem=12, cost=cost(0))


def gather_kernel(parts, stride, *refs):
    pieces, out = refs[:-1], refs[-1]
    here = (lax.axis_index("row") // stride) % parts
    size = pieces[0].shape[0]
    for k, piece in enumerate(pieces):
        at = pl.multiple_of((here ^ k) * size, size)
        value = piece[...].astype(out.dtype)
        out[pl.ds(at, size), :] = value


def gather(stride, pieces, dtype=bf16):
    parts = len(pieces)
    rows, width = pieces[0].shape
    return kernel_call(
        functools.partial(gather_kernel, parts, stride),
        jax.ShapeDtypeStruct((parts * rows, width), dtype), *pieces, vmem=16,
        cost=cost(0),
    )


def local(row_emb, col_emb, counts, row_totals, col_totals, row_ids, col_ids):
    owners = lax.axis_size("row")
    cols_n = lax.axis_size("col")
    block, width = row_emb.shape
    block_cols = col_emb.shape[0]
    steps = counts.shape[0]
    p = Plan(owners, steps, block, width)
    scale = (steps * math.sqrt(owners * block * cols_n * block_cols)) ** (-0.5)

    def row_swap(x, mask):
        return lax.ppermute(x, "row", [(i, i ^ mask) for i in range(owners)])

    def col_swap(x, mask=1):
        return lax.ppermute(x, "col", [(i, i ^ mask) for i in range(cols_n)])

    def grid_swap(x, mask_of):
        perm = []
        for i in range(owners):
            for j in range(cols_n):
                row_mask, col_mask = mask_of(2 * (i % 2) + j % 2)
                perm.append((i * cols_n + j, (i ^ row_mask) * cols_n + (j ^ col_mask)))
        return lax.ppermute(x, ("row", "col"), perm)

    def tie(x, *others):
        return lax.optimization_barrier((x, *others))[0]

    def carry(x, group):
        return grid_swap(x, lambda t: (2 * ((4 * group) ^ turn(t)), 0))

    ids = row_ids.reshape(steps, owners * block // 128, 128)
    totals = row_totals.reshape(1, block)
    msgs = fetch(p, ids, row_emb, row_swap(row_emb, 1), totals, row_swap(totals, 1))
    far = [carry(msgs[3 + g], g) for g in range(1, p.groups)]
    near = [msgs[0]] + [row_swap(msgs[k], 2 * k) for k in range(1, 4)]
    cols, col_logs, index = columns(
        p, col_ids, col_emb, col_totals.reshape(1, block_cols), ids, (msgs[0],)
    )

    every = tuple(range(steps))
    factor = []
    last = (col_logs,)
    term = ()
    sums = []
    for s in every:
        factor += factors(p, scale, counts, s, last, 44 if s == 0 else 38)
        if s == 0:
            *term, total = grads(p, scale, 0, (s,), near, cols, col_logs, factor)
            sums.append(total)
        last = (factor[-1],)
        if s == 0:
            far = [tie(x, *(sums or last), *near[1:]) for x in far]
            last = (*last, *far)
    near[1] = tie(near[1], *last)
    rest = every[len(sums) :]
    term = grads(p, scale, 0, rest, near, cols, col_logs, factor[2 * len(sums) :], (), tuple(term))
    sums += term[3:]
    terms = [term[:3]]
    acc0 = sums[-1]
    crossed = []
    for g in range(1, p.groups):
        here = far[g - 1]
        there = tie(col_swap(here), acc0)
        crossed.append(there)
        four = (here, there, row_swap(pack(here, there), 1))
        made = grads(p, scale, g, every, four, cols, col_logs, factor, tuple(sums))
        terms.append(made[:3])
        sums = made[3:]

    met = [col_swap(t[2] if g else tie(t[2], *crossed)) for g, t in enumerate(terms)]
    placed = ()
    for s in every:
        placed = place(s, s + 1 == steps, col_ids, sums[s], placed)
    mine, *parts = placed
    mine, *others = spread(p.wide, 2, mine, [row_swap(x, 1) for x in parts])
    parcels = []
    for g, (own, passed, _) in enumerate(terms):
        own, passed = meet(own, passed, met[g], () if g else placed[:1])
        parcels.append(merge(p, own, row_swap(passed, 1)))
    (piece,) = spread(1, 1, mine, [row_swap(x, (k + 1) * 2) for k, x in enumerate(others)])
    heres = [carry(x, g) for g, x in enumerate(parcels)]
    theres = [col_swap(x) for x in heres]

    stride = 2 * p.wide
    while stride < owners:
        piece = add(piece, row_swap(piece, stride))
        stride *= 2
    piece = gather(2, [piece] + [row_swap(piece, k * 2) for k in range(1, p.wide)])

    rows = None
    for g, (here, there) in enumerate(zip(heres, theres)):
        rows = collect(p, 4 * g, every, index, (here, there), rows)
        other = row_swap(pack(here, there), 1)
        if g + 1 < p.groups:
            rows = collect(p, 4 * g + 2, every, index, (other, other), rows)
    last = 4 * p.groups - 2
    rows, grad_cols = finish(p, last, every, index, (other, other), rows, piece, row_swap(piece, 1))

    if cols_n > 2:
        total = rows
        for mask in range(2, cols_n, 2):
            total = total + col_swap(rows.astype(bf16), mask).astype(f32)
        rows = total
    return rows, grad_cols


def solution(mesh):
    in_specs = (
        P("row", None),
        P("col", None),
        P(None, "row", "col"),
        P("row"),
        P("col"),
        P(),
        P(None, "col"),
    )
    out_specs = (P("row", None), P("col", None))
    return jax.shard_map(local, mesh=mesh, in_specs=in_specs, out_specs=out_specs, check_vma=False)
```
